512 devices in a mesh: seq: 64 (over x, z), head: 8 (over y, core).
Axes of the slice: x: 4, y: 4, z: 16, core: 2. Of those that a mesh axis runs over, the one named last changes fastest.
Arguments:
- queries: bfloat16 [8192, 16, 128], P('seq', 'head'), may hold values from -21 to 21
- seq_keys: bfloat16 [8192, 16, 128], P('seq', 'head'), may hold values from -6 to 6
- seq_values: bfloat16 [8192, 16, 128], P('seq', 'head'), may hold values from -24 to 24
- memory_keys: bfloat16 [8192, 16, 128], P('seq', 'head'), may hold values from -6 to 6
- memory_values: bfloat16 [8192, 16, 128], P('seq', 'head'), may hold values from -24 to 24
- retrieval: int32 [64, 8], P('seq'), may hold values from 0 to 63, all different within a row
- fifo_head: int32 [1], replicated, may hold values from 0 to 63
- head_gate: float32 [16], P('head'), may hold values from -2 to 2
- norm_gain: float32 [16, 128], P('head'), may hold values from 0.1 to 1.9
Outputs:
- attended: bfloat16 [8192, 16, 128], P('seq', 'head')
The draws below stay inside these ranges and needn't reach their ends.
Inputs may be any that keep to these rules, and one draw needn't show every extreme that they name: `retrieval`: each row names 8 different memory blocks.
All inputs are finite; a program needn't handle non-finite values.
Results may differ from the reference program's by a relative error of at most 0.029.
Values may be sent and summed in bfloat16 or wider, within the bound.
No kernel may reach another device: no remote copies, remote signals or barrier semaphores. Data moves between devices by JAX's collectives and lax.ppermute only.
A program may use at most 128 MiB of HBM per device.

```python
import jax
import jax.numpy as jnp
from jax import lax

HEADS = 16
DH = 128
TOK_DEV = 128
MBLK = 128
TOPK = 8
EXPIRED = 4
TOKENS = 8192
MBLOCKS = 64
N_SEQ = 64


def draw_queries(key, part):
    key = jax.random.fold_in(key, 11)
    drawn = 2.0 * jax.random.normal(key, (TOKENS, HEADS, DH), jnp.float32)
    return jnp.clip(drawn, -12.0, 12.0).astype(jnp.bfloat16)


def draw_seq_keys(key, part):
    key = jax.random.fold_in(key, 12)
    drawn = jax.random.normal(key, (TOKENS, HEADS, DH), jnp.float32)
    return jnp.clip(drawn, -6.0, 6.0).astype(jnp.bfloat16)


def draw_memory_keys(key, part):
    key = jax.random.fold_in(key, 13)
    drawn = jax.random.normal(key, (TOKENS, HEADS, DH), jnp.float32)
    return jnp.clip(drawn, -6.0, 6.0).astype(jnp.bfloat16)


def levels(key, extent, pieces, smallest, largest):
    def one(position, shards_of):
        draws = jax.random.uniform(jax.random.fold_in(jax.random.fold_in(key, 6), position), (shards_of,), jnp.float32, smallest / len(pieces), largest / len(pieces))
        return jnp.repeat(jnp.exp(draws), extent[position] // shards_of).reshape((-1,) + (1,) * (len(extent) - position - 1))

    factor_of = one(*pieces[0])
    for cut in pieces[1:]:
        factor_of = factor_of * one(*cut)
    return factor_of


def choose_distinct(own_key, rows, count, top, lift):
    ranking = jax.random.permutation(jax.random.fold_in(own_key, 1), count)
    favour = ranking
    for power in range(3):
        favour = favour * favour // count
    favour = favour * lift // count
    lots = jax.random.randint(jax.random.fold_in(own_key, 2), (rows, count), 0, 4096) + favour
    sure = jax.random.permutation(jax.random.fold_in(own_key, 3), rows)[jnp.arange(count) % rows]
    lots = jnp.where(jnp.arange(rows)[:, None] == sure[None, :], 1 << 14, lots)
    merit = lots * count + jnp.arange(count)
    return lax.top_k(merit.astype(jnp.int32), top)[1].astype(jnp.int32)


def bell_draw(rng, dims, scale, most, cuts=(), held_as=jnp.bfloat16):
    entries = scale * jax.random.normal(rng, dims, jnp.float32)
    if cuts:
        entries = entries * levels(rng, dims, cuts, -0.22, 0.18)
    return jnp.clip(entries, -most, most).astype(held_as)


def setup_inputs(seed: int = 0) -> dict:
    key_list = jax.random.split(jax.random.key(seed), 10)
    queries = draw_queries(jax.random.fold_in(key_list[9], 71), 0)
    seq_keys = draw_seq_keys(jax.random.fold_in(key_list[9], 71), 0)
    seq_values = bell_draw(key_list[2], (TOKENS, HEADS, DH), 4.0, 24.0, ((0, 64), (1, 8)))
    memory_keys = draw_memory_keys(jax.random.fold_in(key_list[9], 71), 0)
    memory_values = bell_draw(key_list[4], (TOKENS, HEADS, DH), 4.0, 24.0, ((0, 64), (1, 8)))
    retrieval = choose_distinct(key_list[5], N_SEQ, MBLOCKS, TOPK, 2048)
    fifo_head = jax.random.randint(key_list[6], (1,), 0, MBLOCKS).astype(jnp.int32)
    head_gate = jnp.clip(jax.random.uniform(key_list[7], (HEADS,), jnp.float32, -2.0, 2.0) * levels(key_list[7], (HEADS,), ((0, 8),), -0.4, 0.0), -2.0, 2.0)
    norm_gain = jnp.clip(1.0 + 0.18 * jax.random.normal(key_list[8], (HEADS, DH), jnp.float32), 0.1, 1.9)
    return {"queries": queries, "seq_keys": seq_keys, "seq_values": seq_values, "memory_keys": memory_keys, "memory_values": memory_values, "retrieval": retrieval, "fifo_head": fifo_head, "head_gate": head_gate, "norm_gain": norm_gain}


def attend_block(query_rows, key_rows, value_rows, key_mask):
    scores = jnp.einsum('thd,shd->hts', query_rows.astype(jnp.float32), key_rows.astype(jnp.float32)) * DH ** (-0.5)
    scores = jnp.where(key_mask[None], scores, -1e+30)
    row_max = lax.optimization_barrier(jnp.max(scores, -1, keepdims=True))
    exp_scores = jnp.where(key_mask[None], jnp.exp(scores - row_max), 0.0)
    weight_sum = lax.optimization_barrier(jnp.sum(exp_scores, -1))
    rounded = lax.optimization_barrier(exp_scores.astype(jnp.bfloat16)).astype(jnp.float32)
    weighted = jnp.einsum('hts,shd->thd', rounded, value_rows.astype(jnp.float32))
    return weighted / jnp.transpose(weight_sum)[:, :, None]

def reference(queries, seq_keys, seq_values, memory_keys, memory_values, retrieval, fifo_head, head_gate, norm_gain):
    block_count = TOKENS // MBLK
    key_pos = jnp.arange(TOKENS, dtype=jnp.int32)
    block_ids = key_pos // MBLK
    is_live = jnp.mod(block_ids - fifo_head[0] + block_count, block_count) >= EXPIRED
    gate_mix = jax.nn.sigmoid(head_gate)[None, :, None]

    def one_block(block_index):
        first_row = (block_index * TOK_DEV).astype(jnp.int32)
        query_rows = lax.dynamic_slice_in_dim(queries, first_row, TOK_DEV, 0)
        query_pos = first_row + jnp.arange(TOK_DEV, dtype=jnp.int32)
        causal = key_pos[None, :] <= query_pos[:, None]
        local_out = attend_block(query_rows, seq_keys, seq_values, causal)
        wanted = retrieval[block_index]
        chosen = jnp.any(block_ids[:, None] == wanted[None, :], -1) & is_live
        memory_mask = jnp.broadcast_to(chosen[None, :], (TOK_DEV, TOKENS))
        memory_out = attend_block(query_rows, memory_keys, memory_values, memory_mask)
        return gate_mix * memory_out + (1.0 - gate_mix) * local_out
    combined = lax.map(one_block, jnp.arange(N_SEQ, dtype=jnp.int32))
    combined = combined.reshape(TOKENS, HEADS, DH)
    mean_square = lax.optimization_barrier(jnp.mean(combined * combined, axis=(1, 2), keepdims=True))
    return (combined * lax.rsqrt(mean_square + 1e-06) * norm_gain[None]).astype(jnp.bfloat16)
```

```python
import jax
import jax.numpy as jnp
from jax import lax
from jax.experimental import pallas as pl
from jax.experimental.pallas import tpu as pltpu
from jax.sharding import PartitionSpec as P

HEADS = 16
DH = 128
TOK = 128
EXPIRED = 4
BLOCKS = 64
NX, NZ = 4, 16
NR = 8
NC = 8
QROWS = 2 * TOK + 16
OROWS = 4 * DH + 16
NEG = -1e30
FLOOR = -1e29
LOG2_SCALE = DH**-0.5 * 1.4426950408889634

R_GROUPS = [[x * NZ + 2 * r + par for r in range(NR)] for x in range(NX) for par in range(2)]
C_GROUPS = [[x * NZ + 2 * k + par for x in range(NX) for par in range(2)] for k in range(NZ // 2)]

NT = (((1,), (1,)), ((), ()))
NN = (((1,), (0,)), ((), ()))


def dot(a, b, dims):
    return lax.dot_general(a, b, dims, preferred_element_type=jnp.float32)


def split_perm():
    row = lax.broadcasted_iota(jnp.int32, (2 * TOK, 2 * TOK), 0)
    col = lax.broadcasted_iota(jnp.int32, (2 * TOK, 2 * TOK), 1)
    source = (row % TOK) * 2 + row // TOK
    return jnp.where(col == source, 1.0, 0.0).astype(jnp.bfloat16)


def prep_kernel(want_ref, fifo_ref, q_ref, k_ref, v_ref, mk_ref, mv_ref, kv_out, q_out):
    perm = split_perm()
    for place, ref in ((0, k_ref), (2, mk_ref)):
        kv_out[pl.ds(place * 256, 256), :] = dot(perm, ref[...], NN).astype(jnp.bfloat16)
    for place, ref in ((1, v_ref), (3, mv_ref)):
        rows = dot(perm, ref[...], NN)
        for h in range(2):
            block = jnp.transpose(rows[h * TOK : (h + 1) * TOK, :])
            kv_out[pl.ds(place * 256 + h * TOK, TOK), :] = block.astype(jnp.bfloat16)
    q_rows = dot(perm, q_ref[...], NN).astype(jnp.bfloat16)
    row = lax.broadcasted_iota(jnp.int32, (16, TOK), 0)
    for c in range(NC):
        q_out[c, pl.ds(0, 2 * TOK), :] = q_rows
        block = (c // 2) * NZ + 2 * row + c % 2
        chosen = block == want_ref[0, 0]
        for i in range(1, 8):
            chosen = chosen | (block == want_ref[0, i])
        live = ((block - fifo_ref[0] + BLOCKS) & (BLOCKS - 1)) >= EXPIRED
        q_out[c, pl.ds(2 * TOK, 16), :] = jnp.where(chosen & live, 0.0, NEG).astype(jnp.bfloat16)


def attend_kernel(pos_ref, q_ref, kv_ref, out_ref):
    my_x, my_pair, my_par = pos_ref[0], pos_ref[1], pos_ref[2]
    ahead = lax.broadcasted_iota(jnp.int32, (TOK, 2 * TOK), 0) - lax.broadcasted_iota(
        jnp.int32, (TOK, 2 * TOK), 1
    )

    def step(xq, carry):
        stats = []
        extra = [q_ref[2 * xq + par, pl.ds(2 * TOK, 16), :].astype(jnp.float32) for par in range(2)]
        bias = jnp.concatenate(extra, 1)
        for kind in range(2):
            for h in range(2):
                q_rows = jnp.concatenate(
                    [q_ref[2 * xq + par, pl.ds(h * TOK, TOK), :] for par in range(2)], 0
                )
                scores = []
                for r in range(NR):
                    keys = kv_ref[r, pl.ds(kind * 512 + h * TOK, TOK), :]
                    s = dot(keys, q_rows, NT)
                    if kind == 0:
                        gap = ((xq - my_x) * NZ + 2 * my_pair - 2 * r - my_par) * TOK
                        s = jnp.where(ahead <= gap, s, NEG)
                    else:
                        s = s + bias[r : r + 1, :]
                    scores.append(s)
                s = jnp.concatenate(scores, 0)
                top = jnp.maximum(jnp.max(s, 0, keepdims=True), FLOOR) * LOG2_SCALE
                e = jnp.exp2(s * LOG2_SCALE - top)
                total = jnp.sum(e, 0, keepdims=True)
                total = jnp.maximum(total, 1e-30)
                vals = jnp.concatenate(
                    [kv_ref[r, pl.ds(kind * 512 + 256 + h * TOK, TOK), :] for r in range(NR)], 1
                )
                acc = dot(vals, e.astype(jnp.bfloat16), NN) * (1.0 / total)
                acc = acc.astype(jnp.bfloat16)
                for par in range(2):
                    out_ref[2 * xq + par, pl.ds((kind * 2 + h) * DH, DH), :] = acc[
                        :, par * TOK : (par + 1) * TOK
                    ]
                lse = top + jnp.log2(total)
                for _ in range(3):
                    part = lse.astype(jnp.bfloat16).astype(jnp.float32)
                    stats.append(part)
                    lse = lse - part
        stats.append(jnp.zeros((4, 2 * TOK), jnp.float32))
        tile = jnp.concatenate(stats, 0).astype(jnp.bfloat16)
        for par in range(2):
            out_ref[2 * xq + par, pl.ds(4 * DH, 16), :] = tile[:, par * TOK : (par + 1) * TOK]
        return carry

    lax.fori_loop(0, NX, step, 0)


def merge_kernel(gate_ref, part_ref, comb_ref, sq_ref):
    stats = [part_ref[c, pl.ds(4 * DH, 16), :].astype(jnp.float32) for c in range(NC)]
    squares = jnp.zeros((1, TOK), jnp.float32)
    for h in range(2):
        merged = []
        for kind in range(2):
            at = (kind * 2 + h) * 3
            lse = [st[at : at + 1] + st[at + 1 : at + 2] + st[at + 2 : at + 3] for st in stats]
            top = lse[0]
            for one in lse[1:]:
                top = jnp.maximum(top, one)
            weight = [jnp.exp2(one - top) for one in lse]
            total = weight[0]
            for one in weight[1:]:
                total = total + one
            acc = jnp.zeros((DH, TOK), jnp.float32)
            for c in range(NC):
                rows = part_ref[c, pl.ds((kind * 2 + h) * DH, DH), :].astype(jnp.float32)
                acc = acc + rows * weight[c]
            merged.append(acc * (1.0 / total))
        gate = gate_ref[h : h + 1, :]
        comb = gate * merged[1] + (1.0 - gate) * merged[0]
        comb_ref[h] = comb
        squares = squares + jnp.sum(comb * comb, 0, keepdims=True)
    sq_ref[...] = jnp.broadcast_to(squares, (8, TOK))


def final_kernel(sq_ref, comb_ref, gain_ref, out_ref):
    mean_square = jnp.sum(sq_ref[...], 0, keepdims=True) * (1.0 / (HEADS * DH))
    scale = lax.rsqrt(mean_square + 1e-06)
    diag = lax.broadcasted_iota(jnp.int32, (DH, DH), 0) == lax.broadcasted_iota(jnp.int32, (DH, DH), 1)
    cols = []
    for h in range(2):
        gain = jnp.sum(jnp.where(diag, gain_ref[h : h + 1, :], 0.0), 1, keepdims=True)
        cols.append((comb_ref[h] * scale * gain).astype(jnp.bfloat16))
    row = lax.broadcasted_iota(jnp.int32, (2 * TOK, 2 * TOK), 0)
    col = lax.broadcasted_iota(jnp.int32, (2 * TOK, 2 * TOK), 1)
    pick = jnp.where(col == (row % 2) * TOK + row // 2, 1.0, 0.0).astype(jnp.bfloat16)
    out_ref[...] = dot(pick, jnp.concatenate(cols, 1), NT).astype(jnp.bfloat16)


VMEM = pl.BlockSpec(memory_space=pltpu.VMEM)
SMEM = pl.BlockSpec(memory_space=pltpu.SMEM)
PARAMS = pltpu.CompilerParams(vmem_limit_bytes=40 * 2**20)


def on_device(queries, seq_keys, seq_values, memory_keys, memory_values, retrieval, fifo_head, head_gate, norm_gain):
    me = lax.axis_index("seq")
    pos = jnp.stack([me // NZ, (me % NZ) // 2, me % 2]).astype(jnp.int32)
    flat = lambda a: a.reshape(2 * TOK, DH)
    kv, q_parts = pl.pallas_call(
        prep_kernel,
        out_shape=(
            jax.ShapeDtypeStruct((1024, DH), jnp.bfloat16),
            jax.ShapeDtypeStruct((NC, QROWS, DH), jnp.bfloat16),
        ),
        in_specs=[SMEM, SMEM] + [VMEM] * 5,
        out_specs=(VMEM, VMEM),
        compiler_params=PARAMS,
        name="prep",
    )(retrieval, fifo_head, *map(flat, (queries, seq_keys, seq_values, memory_keys, memory_values)))
    kv_all = lax.all_gather(kv, "seq", axis_index_groups=R_GROUPS)
    q_all = lax.all_to_all(q_parts, "seq", 0, 0, axis_index_groups=C_GROUPS, tiled=True)
    parts = pl.pallas_call(
        attend_kernel,
        out_shape=jax.ShapeDtypeStruct((NC, OROWS, DH), jnp.bfloat16),
        in_specs=[SMEM, VMEM, VMEM],
        out_specs=VMEM,
        compiler_params=PARAMS,
        name="attend",
    )(pos, q_all, kv_all)
    parts = lax.all_to_all(parts, "seq", 0, 0, axis_index_groups=C_GROUPS, tiled=True)
    gate = jnp.broadcast_to(jax.nn.sigmoid(head_gate)[:, None], (2, TOK))
    comb, squares = pl.pallas_call(
        merge_kernel,
        out_shape=(
            jax.ShapeDtypeStruct((2, DH, TOK), jnp.float32),
            jax.ShapeDtypeStruct((8, TOK), jnp.float32),
        ),
        in_specs=[VMEM, VMEM],
        out_specs=(VMEM, VMEM),
        compiler_params=PARAMS,
        name="merge",
    )(gate, parts)
    squares = lax.all_to_all(squares, "head", 0, 0, tiled=True)
    out = pl.pallas_call(
        final_kernel,
        out_shape=jax.ShapeDtypeStruct((2 * TOK, DH), jnp.bfloat16),
        in_specs=[VMEM] * 3,
        out_specs=VMEM,
        compiler_params=PARAMS,
        name="final",
    )(squares, comb, norm_gain)
    return out.reshape(TOK, 2, DH)


def solution(mesh):
    in_specs = (P("seq", "head", None),) * 5 + (P("seq", None), P(), P("head"), P("head", None))
    return jax.shard_map(
        on_device, mesh=mesh, in_specs=in_specs, out_specs=P("seq", "head", None), check_vma=False
    )
```

```python
import jax
import jax.numpy as jnp
from jax import lax
from jax.experimental import pallas as pl
from jax.experimental.pallas import tpu as pltpu
from jax.sharding import PartitionSpec as P

HEADS = 16
DH = 128
TOK = 128
EXPIRED = 4
BLOCKS = 64
NX, NZ = 4, 16
NR = 8
NC = 8
QROWS = 2 * TOK + 16
OROWS = 4 * DH + 16
KVROWS = 8 * TOK + 16
NEG = -1e30
FLOOR = -1e29
LOG2_SCALE = DH**-0.5 * 1.4426950408889634

R_GROUPS = [[x * NZ + 2 * r + par for r in range(NR)] for x in range(NX) for par in range(2)]
C_GROUPS = [[x * NZ + 2 * k + par for x in range(NX) for par in range(2)] for k in range(NZ // 2)]

NT = (((1,), (1,)), ((), ()))
NN = (((1,), (0,)), ((), ()))


def dot(a, b, dims):
    return lax.dot_general(a, b, dims, preferred_element_type=jnp.float32)


def split_perm():
    row = lax.broadcasted_iota(jnp.int32, (2 * TOK, 2 * TOK), 0)
    col = lax.broadcasted_iota(jnp.int32, (2 * TOK, 2 * TOK), 1)
    source = (row % TOK) * 2 + row // TOK
    return jnp.where(col == source, 1.0, 0.0).astype(jnp.bfloat16)


def query_kernel(want_hbm, fifo_hbm, q_hbm, q_out, want, fifo, q_in, sems):
    copies = [
        pltpu.make_async_copy(src, dst, sems.at[i])
        for i, (src, dst) in enumerate(((want_hbm, want), (fifo_hbm, fifo), (q_hbm, q_in)))
    ]
    for copy in copies:
        copy.start()
    perm = split_perm()
    for copy in copies:
        copy.wait()
    q_rows = dot(perm, q_in[...], NN).astype(jnp.bfloat16)
    row = lax.broadcasted_iota(jnp.int32, (16, TOK), 0)
    for c in range(NC):
        q_out[c, pl.ds(0, 2 * TOK), :] = q_rows
        block = (c // 2) * NZ + 2 * row + c % 2
        chosen = block == want[0, 0]
        for i in range(1, 8):
            chosen = chosen | (block == want[0, i])
        live = ((block - fifo[0] + BLOCKS) & (BLOCKS - 1)) >= EXPIRED
        q_out[c, pl.ds(2 * TOK, 16), :] = jnp.where(chosen & live, 0.0, NEG).astype(jnp.bfloat16)


def code_kernel(k_hbm, v_hbm, mk_hbm, mv_hbm, kv_out, rows_in, sems):
    copies = [
        pltpu.make_async_copy(src, rows_in.at[i], sems.at[i])
        for i, src in enumerate((k_hbm, v_hbm, mk_hbm, mv_hbm))
    ]
    for copy in copies:
        copy.start()
    perm = split_perm()
    powers = []
    for i, copy in enumerate(copies):
        copy.wait()
        rows = dot(perm, rows_in[i], NN)
        for h in range(2):
            block = rows[h * TOK : (h + 1) * TOK, :]
            if i % 2:
                block = jnp.transpose(block)
            peak = jnp.max(jnp.max(jnp.abs(block), 0, keepdims=True), 1, keepdims=True)
            power = jnp.floor(14.999 - jnp.log2(jnp.maximum(peak, 1e-30)))
            power = jnp.broadcast_to(power, (1, TOK))
            code = jnp.floor(block * jnp.exp2(power) + 0.5).astype(jnp.int32)
            kv_out[pl.ds((i * 2 + h) * TOK, TOK), :] = code.astype(jnp.int16)
            powers.append(power)
    powers.append(jnp.zeros((8, TOK), jnp.float32))
    tile = jnp.concatenate(powers, 0).astype(jnp.int32)
    kv_out[pl.ds(8 * TOK, 16), :] = tile.astype(jnp.int16)


def decode(kv_ref, keys_ref, vals_ref):
    for r in range(NR):
        power = kv_ref[r, pl.ds(8 * TOK, 16), :].astype(jnp.int32).astype(jnp.float32)
        factor = jnp.exp2(-power)
        for i in range(4):
            for h in range(2):
                code = kv_ref[r, pl.ds((i * 2 + h) * TOK, TOK), :].astype(jnp.int32)
                block = code.astype(jnp.float32) * factor[i * 2 + h : i * 2 + h + 1, :]
                block = block.astype(jnp.bfloat16)
                at = (i // 2) * 2 + h
                if i % 2:
                    vals_ref[at, :, pl.ds(r * TOK, TOK)] = block
                else:
                    keys_ref[at, pl.ds(r * TOK, TOK), :] = block


def attend_kernel(pos_ref, q_ref, kv_ref, out_ref, keys_ref, vals_ref):
    decode(kv_ref, keys_ref, vals_ref)
    my_x, my_pair, my_par = pos_ref[0], pos_ref[1], pos_ref[2]
    ahead = lax.broadcasted_iota(jnp.int32, (TOK, 2 * TOK), 0) - lax.broadcasted_iota(
        jnp.int32, (TOK, 2 * TOK), 1
    )

    def step(xq, carry):
        stats = []
        extra = [q_ref[2 * xq + par, pl.ds(2 * TOK, 16), :].astype(jnp.float32) for par in range(2)]
        bias = jnp.concatenate(extra, 1)
        for kind in range(2):
            for h in range(2):
                q_rows = jnp.concatenate(
                    [q_ref[2 * xq + par, pl.ds(h * TOK, TOK), :] for par in range(2)], 0
                )
                scores = []
                for r in range(NR):
                    keys = keys_ref[kind * 2 + h, pl.ds(r * TOK, TOK), :]
                    s = dot(keys, q_rows, NT)
                    if kind == 0:
                        gap = ((xq - my_x) * NZ + 2 * my_pair - 2 * r - my_par) * TOK
                        s = jnp.where(ahead <= gap, s, NEG)
                    else:
                        s = s + bias[r : r + 1, :]
                    scores.append(s)
                s = jnp.concatenate(scores, 0)
                top = jnp.maximum(jnp.max(s, 0, keepdims=True), FLOOR) * LOG2_SCALE
                e = jnp.exp2(s * LOG2_SCALE - top)
                total = jnp.sum(e, 0, keepdims=True)
                total = jnp.maximum(total, 1e-30)
                acc = dot(vals_ref[kind * 2 + h], e.astype(jnp.bfloat16), NN) * (1.0 / total)
                acc = acc.astype(jnp.bfloat16)
                for par in range(2):
                    out_ref[2 * xq + par, pl.ds((kind * 2 + h) * DH, DH), :] = acc[
                        :, par * TOK : (par + 1) * TOK
                    ]
                lse = top + jnp.log2(total)
                for _ in range(3):
                    part = lse.astype(jnp.bfloat16).astype(jnp.float32)
                    stats.append(part)
                    lse = lse - part
        stats.append(jnp.zeros((4, 2 * TOK), jnp.float32))
        tile = jnp.concatenate(stats, 0).astype(jnp.bfloat16)
        for par in range(2):
            out_ref[2 * xq + par, pl.ds(4 * DH, 16), :] = tile[:, par * TOK : (par + 1) * TOK]
        return carry

    lax.fori_loop(0, NX, step, 0)


def merge_kernel(gate_ref, part_ref, comb_ref, sq_ref):
    stats = [part_ref[c, pl.ds(4 * DH, 16), :].astype(jnp.float32) for c in range(NC)]
    squares = jnp.zeros((1, TOK), jnp.float32)
    for h in range(2):
        merged = []
        for kind in range(2):
            at = (kind * 2 + h) * 3
            lse = [st[at : at + 1] + st[at + 1 : at + 2] + st[at + 2 : at + 3] for st in stats]
            top = lse[0]
            for one in lse[1:]:
                top = jnp.maximum(top, one)
            weight = [jnp.exp2(one - top) for one in lse]
            total = weight[0]
            for one in weight[1:]:
                total = total + one
            acc = jnp.zeros((DH, TOK), jnp.float32)
            for c in range(NC):
                rows = part_ref[c, pl.ds((kind * 2 + h) * DH, DH), :].astype(jnp.float32)
                acc = acc + rows * weight[c]
            merged.append(acc * (1.0 / total))
        gate = gate_ref[h : h + 1, :]
        comb = gate * merged[1] + (1.0 - gate) * merged[0]
        comb_ref[h] = comb
        squares = squares + jnp.sum(comb * comb, 0, keepdims=True)
    sq_ref[...] = jnp.broadcast_to(squares, (8, TOK))


def final_kernel(sq_ref, comb_ref, gain_ref, out_ref):
    mean_square = jnp.sum(sq_ref[...], 0, keepdims=True) * (1.0 / (HEADS * DH))
    scale = lax.rsqrt(mean_square + 1e-06)
    diag = lax.broadcasted_iota(jnp.int32, (DH, DH), 0) == lax.broadcasted_iota(jnp.int32, (DH, DH), 1)
    cols = []
    for h in range(2):
        gain = jnp.sum(jnp.where(diag, gain_ref[h : h + 1, :], 0.0), 1, keepdims=True)
        cols.append((comb_ref[h] * scale * gain).astype(jnp.bfloat16))
    row = lax.broadcasted_iota(jnp.int32, (2 * TOK, 2 * TOK), 0)
    col = lax.broadcasted_iota(jnp.int32, (2 * TOK, 2 * TOK), 1)
    pick = jnp.where(col == (row % 2) * TOK + row // 2, 1.0, 0.0).astype(jnp.bfloat16)
    out_ref[...] = dot(pick, jnp.concatenate(cols, 1), NT).astype(jnp.bfloat16)


VMEM = pl.BlockSpec(memory_space=pltpu.VMEM)
ANY = pl.BlockSpec(memory_space=pl.ANY)
SMEM = pl.BlockSpec(memory_space=pltpu.SMEM)
PARAMS = pltpu.CompilerParams(vmem_limit_bytes=40 * 2**20)


def on_device(queries, seq_keys, seq_values, memory_keys, memory_values, retrieval, fifo_head, head_gate, norm_gain):
    me = lax.axis_index("seq")
    pos = jnp.stack([me // NZ, (me % NZ) // 2, me % 2]).astype(jnp.int32)
    flat = lambda a: a.reshape(2 * TOK, DH)
    q_parts = pl.pallas_call(
        query_kernel,
        out_shape=jax.ShapeDtypeStruct((NC, QROWS, DH), jnp.bfloat16),
        in_specs=[ANY] * 3,
        out_specs=VMEM,
        scratch_shapes=[
            pltpu.SMEM((1, 8), jnp.int32),
            pltpu.SMEM((1,), jnp.int32),
            pltpu.VMEM((2 * TOK, DH), jnp.bfloat16),
            pltpu.SemaphoreType.DMA((3,)),
        ],
        compiler_params=PARAMS,
        name="query",
    )(retrieval, fifo_head, flat(queries))
    q_all = lax.all_to_all(q_parts, "seq", 0, 0, axis_index_groups=C_GROUPS, tiled=True)
    kv = pl.pallas_call(
        code_kernel,
        out_shape=jax.ShapeDtypeStruct((KVROWS, DH), jnp.int16),
        in_specs=[ANY] * 4,
        out_specs=VMEM,
        scratch_shapes=[
            pltpu.VMEM((4, 2 * TOK, DH), jnp.bfloat16),
            pltpu.SemaphoreType.DMA((4,)),
        ],
        compiler_params=PARAMS,
        name="code",
    )(*map(flat, (seq_keys, seq_values, memory_keys, memory_values)))
    kv_all = lax.all_gather(kv, "seq", axis_index_groups=R_GROUPS)
    parts = pl.pallas_call(
        attend_kernel,
        out_shape=jax.ShapeDtypeStruct((NC, OROWS, DH), jnp.bfloat16),
        in_specs=[SMEM, VMEM, VMEM],
        out_specs=VMEM,
        scratch_shapes=[
            pltpu.VMEM((4, NR * TOK, DH), jnp.bfloat16),
            pltpu.VMEM((4, DH, NR * TOK), jnp.bfloat16),
        ],
        compiler_params=PARAMS,
        name="attend",
    )(pos, q_all, kv_all)
    parts = lax.all_to_all(parts, "seq", 0, 0, axis_index_groups=C_GROUPS, tiled=True)
    gate = jnp.broadcast_to(jax.nn.sigmoid(head_gate)[:, None], (2, TOK))
    comb, squares = pl.pallas_call(
        merge_kernel,
        out_shape=(
            jax.ShapeDtypeStruct((2, DH, TOK), jnp.float32),
            jax.ShapeDtypeStruct((8, TOK), jnp.float32),
        ),
        in_specs=[VMEM, VMEM],
        out_specs=(VMEM, VMEM),
        compiler_params=PARAMS,
        name="merge",
    )(gate, parts)
    squares = lax.all_to_all(squares, "head", 0, 0, tiled=True)
    out = pl.pallas_call(
        final_kernel,
        out_shape=jax.ShapeDtypeStruct((2 * TOK, DH), jnp.bfloat16),
        in_specs=[VMEM] * 3,
        out_specs=VMEM,
        compiler_params=PARAMS,
        name="final",
    )(squares, comb, norm_gain)
    return out.reshape(TOK, 2, DH)


def solution(mesh):
    in_specs = (P("seq", "head", None),) * 5 + (P("seq", None), P(), P("head"), P("head", None))
    return jax.shard_map(
        on_device, mesh=mesh, in_specs=in_specs, out_specs=P("seq", "head", None), check_vma=False
    )
```

```python
import jax
import jax.numpy as jnp
from jax import lax
from jax.experimental import pallas as pl
from jax.experimental.pallas import tpu as pltpu
from jax.sharding import PartitionSpec as P

HEADS = 16
DH = 128
TOK = 128
EXPIRED = 4
BLOCKS = 64
NX, NZ = 4, 16
NR = 8
NC = 8
QROWS = 2 * TOK + 16
OROWS = 4 * DH + 16
KVROWS = 8 * TOK + 16
NEG = -1e30
FLOOR = -1e29
LOG2_SCALE = DH**-0.5 * 1.4426950408889634

R_GROUPS = [[x * NZ + 2 * r + par for r in range(NR)] for x in range(NX) for par in range(2)]
C_GROUPS = [[x * NZ + 2 * k + par for x in range(NX) for par in range(2)] for k in range(NZ // 2)]

NT = (((1,), (1,)), ((), ()))
NN = (((1,), (0,)), ((), ()))


def dot(a, b, dims):
    return lax.dot_general(a, b, dims, preferred_element_type=jnp.float32)


def split_perm():
    row = lax.broadcasted_iota(jnp.int32, (2 * TOK, 2 * TOK), 0)
    col = lax.broadcasted_iota(jnp.int32, (2 * TOK, 2 * TOK), 1)
    source = (row % TOK) * 2 + row // TOK
    return jnp.where(col == source, 1.0, 0.0).astype(jnp.bfloat16)


def query_kernel(want_hbm, fifo_hbm, q_hbm, q_out, want, fifo, q_in, sems):
    copies = [
        pltpu.make_async_copy(src, dst, sems.at[i])
        for i, (src, dst) in enumerate(((want_hbm, want), (fifo_hbm, fifo), (q_hbm, q_in)))
    ]
    for copy in copies:
        copy.start()
    perm = split_perm()
    for copy in copies:
        copy.wait()
    q_rows = dot(perm, q_in[...], NN).astype(jnp.bfloat16)
    row = lax.broadcasted_iota(jnp.int32, (16, TOK), 0)
    for c in range(NC):
        q_out[c, pl.ds(0, 2 * TOK), :] = q_rows
        block = (c // 2) * NZ + 2 * row + c % 2
        chosen = block == want[0, 0]
        for i in range(1, 8):
            chosen = chosen | (block == want[0, i])
        live = ((block - fifo[0] + BLOCKS) & (BLOCKS - 1)) >= EXPIRED
        q_out[c, pl.ds(2 * TOK, 16), :] = jnp.where(chosen & live, 0.0, NEG).astype(jnp.bfloat16)


def code_kernel(k_hbm, v_hbm, mk_hbm, mv_hbm, kv_out, rows_in, sems):
    copies = [
        pltpu.make_async_copy(src, rows_in.at[i], sems.at[i])
        for i, src in enumerate((k_hbm, v_hbm, mk_hbm, mv_hbm))
    ]
    for copy in copies:
        copy.start()
    perm = split_perm()
    powers = []
    for i, copy in enumerate(copies):
        copy.wait()
        rows = dot(perm, rows_in[i], NN)
        for h in range(2):
            block = rows[h * TOK : (h + 1) * TOK, :]
            if i % 2:
                block = jnp.transpose(block)
            peak = jnp.max(jnp.max(jnp.abs(block), 0, keepdims=True), 1, keepdims=True)
            power = jnp.floor(14.999 - jnp.log2(jnp.maximum(peak, 1e-30)))
            power = jnp.broadcast_to(power, (1, TOK))
            code = jnp.floor(block * jnp.exp2(power) + 0.5).astype(jnp.int32)
            kv_out[pl.ds((i * 2 + h) * TOK, TOK), :] = code.astype(jnp.int16)
            powers.append(power)
    powers.append(jnp.zeros((8, TOK), jnp.float32))
    tile = jnp.concatenate(powers, 0).astype(jnp.int32)
    kv_out[pl.ds(8 * TOK, 16), :] = tile.astype(jnp.int16)


def tok_start(r):
    return r * TOK if isinstance(r, int) else pl.multiple_of(r * TOK, TOK)


def decode(kv_ref, keys_ref, vals_ref):
    for r in range(NR):
        power = kv_ref[r, pl.ds(8 * TOK, 16), :].astype(jnp.int32).astype(jnp.float32)
        factor = jnp.exp2(-power)
        for i in range(4):
            for h in range(2):
                code = kv_ref[r, pl.ds((i * 2 + h) * TOK, TOK), :].astype(jnp.bfloat16)
                block = code * factor[i * 2 + h : i * 2 + h + 1, :].astype(jnp.bfloat16)
                at = (i // 2) * 2 + h
                if i % 2:
                    vals_ref[at, :, pl.ds(r * TOK, TOK)] = block
                else:
                    keys_ref[at, pl.ds(r * TOK, TOK), :] = block


def attend_kernel(
    pos_ref, q_ref, kv_ref, out_ref, keys_ref, vals_ref, s_ref, bias_ref, stat_ref, slot_ref
):
    decode(kv_ref, keys_ref, vals_ref)
    my_x, my_pair, my_par = pos_ref[0], pos_ref[1], pos_ref[2]
    ahead = lax.broadcasted_iota(jnp.int32, (TOK, 2 * TOK), 0) - lax.broadcasted_iota(
        jnp.int32, (TOK, 2 * TOK), 1
    )
    row = lax.broadcasted_iota(jnp.int32, (16, TOK), 0)
    place = jnp.where(row < NR, jnp.left_shift(1, row), 0).astype(jnp.float32)

    def run(xq, kind, blocks, mask):
        tops = []
        for h in range(2):
            at = kind * 2 + h
            q_rows = jnp.concatenate(
                [q_ref[2 * xq + par, pl.ds(h * TOK, TOK), :] for par in range(2)], 0
            )
            top = jnp.full((8, 2 * TOK), FLOOR, jnp.float32)
            for i, r in enumerate(blocks):
                s = mask(i, dot(keys_ref[at, pl.ds(tok_start(r), TOK), :], q_rows, NT))
                s_ref[at, pl.ds(i * TOK, TOK), :] = s
                top = jnp.maximum(top, jnp.max(s.reshape(TOK // 8, 8, 2 * TOK), 0))
            tops.append(jnp.max(top, 0, keepdims=True) * LOG2_SCALE)
        for h in range(2):
            at = kind * 2 + h
            top = tops[h]
            total = jnp.zeros((8, 2 * TOK), jnp.float32)
            acc = jnp.zeros((DH, 2 * TOK), jnp.float32)
            for i in range(0, len(blocks), 2):
                e = jnp.exp2(s_ref[at, pl.ds(i * TOK, 2 * TOK), :] * LOG2_SCALE - top)
                total = total + jnp.sum(e.reshape(2 * TOK // 8, 8, 2 * TOK), 0)
                vals = jnp.concatenate(
                    [vals_ref[at, :, pl.ds(tok_start(r), TOK)] for r in blocks[i : i + 2]], 1
                )
                acc = acc + dot(vals, e.astype(jnp.bfloat16), NN)
            total = jnp.maximum(jnp.sum(total, 0, keepdims=True), 1e-30)
            acc = (acc * (1.0 / total)).astype(jnp.bfloat16)
            for par in range(2):
                out_ref[2 * xq + par, pl.ds(at * DH, DH), :] = acc[:, par * TOK : (par + 1) * TOK]
            lse = top + jnp.log2(total)
            for i in range(3):
                part = lse.astype(jnp.bfloat16).astype(jnp.float32)
                stat_ref[at * 3 + i : at * 3 + i + 1, :] = part
                lse = lse - part

    def step(xq, carry):
        def causal(r, s):
            gap = ((xq - my_x) * NZ + 2 * my_pair - 2 * r - my_par) * TOK
            return jnp.where(ahead <= gap, s, NEG)

        extra = [q_ref[2 * xq + par, pl.ds(2 * TOK, 16), :].astype(jnp.float32) for par in range(2)]
        bias_ref[...] = jnp.concatenate(extra, 1)
        wanted = jnp.where(jnp.maximum(extra[0], extra[1]) > -1.0, place, 0.0)
        bits = jnp.max(jnp.sum(wanted, 0, keepdims=True)).astype(jnp.int32)
        for r in range(NR):
            slot_ref[r] = 0
        count = jnp.int32(0)
        for r in range(NR):
            slot_ref[count] = r
            count = count + (jnp.right_shift(bits, r) & 1)

        run(xq, 0, list(range(NR)), causal)

        def some(size):
            blocks = [slot_ref[i] for i in range(size)]

            def retrieved(i, s):
                return s + jnp.where(i < count, bias_ref[pl.ds(blocks[i], 1), :], NEG)

            run(xq, 1, blocks, retrieved)

        @pl.when(count <= 2)
        def _():
            some(2)

        @pl.when((count > 2) & (count <= 4))
        def _():
            some(4)

        @pl.when(count > 4)
        def _():
            some(8)

        tile = stat_ref[...].astype(jnp.bfloat16)
        for par in range(2):
            out_ref[2 * xq + par, pl.ds(4 * DH, 16), :] = tile[:, par * TOK : (par + 1) * TOK]
        return carry

    stat_ref[...] = jnp.zeros((16, 2 * TOK), jnp.float32)
    lax.fori_loop(0, NX, step, 0)


SCRATCH = [
    pltpu.VMEM((4, NR * TOK, DH), jnp.bfloat16),
    pltpu.VMEM((4, DH, NR * TOK), jnp.bfloat16),
    pltpu.VMEM((4, NR * TOK, 2 * TOK), jnp.float32),
    pltpu.VMEM((16, 2 * TOK), jnp.float32),
    pltpu.VMEM((16, 2 * TOK), jnp.float32),
    pltpu.SMEM((8,), jnp.int32),
]


def merge_kernel(gate_ref, part_ref, comb_ref, sq_ref):
    stats = [part_ref[c, pl.ds(4 * DH, 16), :].astype(jnp.float32) for c in range(NC)]
    squares = jnp.zeros((1, TOK), jnp.float32)
    for h in range(2):
        merged = []
        for kind in range(2):
            at = (kind * 2 + h) * 3
            lse = [st[at : at + 1] + st[at + 1 : at + 2] + st[at + 2 : at + 3] for st in stats]
            top = lse[0]
            for one in lse[1:]:
                top = jnp.maximum(top, one)
            weight = [jnp.exp2(one - top) for one in lse]
            total = weight[0]
            for one in weight[1:]:
                total = total + one
            acc = jnp.zeros((DH, TOK), jnp.float32)
            for c in range(NC):
                rows = part_ref[c, pl.ds((kind * 2 + h) * DH, DH), :].astype(jnp.float32)
                acc = acc + rows * weight[c]
            merged.append(acc * (1.0 / total))
        gate = gate_ref[h : h + 1, :]
        comb = gate * merged[1] + (1.0 - gate) * merged[0]
        comb_ref[h] = comb
        squares = squares + jnp.sum(comb * comb, 0, keepdims=True)
    sq_ref[...] = jnp.broadcast_to(squares, (8, TOK))


def final_kernel(sq_ref, comb_ref, gain_ref, out_ref):
    mean_square = jnp.sum(sq_ref[...], 0, keepdims=True) * (1.0 / (HEADS * DH))
    scale = lax.rsqrt(mean_square + 1e-06)
    diag = lax.broadcasted_iota(jnp.int32, (DH, DH), 0) == lax.broadcasted_iota(jnp.int32, (DH, DH), 1)
    cols = []
    for h in range(2):
        gain = jnp.sum(jnp.where(diag, gain_ref[h : h + 1, :], 0.0), 1, keepdims=True)
        cols.append((comb_ref[h] * scale * gain).astype(jnp.bfloat16))
    row = lax.broadcasted_iota(jnp.int32, (2 * TOK, 2 * TOK), 0)
    col = lax.broadcasted_iota(jnp.int32, (2 * TOK, 2 * TOK), 1)
    pick = jnp.where(col == (row % 2) * TOK + row // 2, 1.0, 0.0).astype(jnp.bfloat16)
    out_ref[...] = dot(pick, jnp.concatenate(cols, 1), NT).astype(jnp.bfloat16)


VMEM = pl.BlockSpec(memory_space=pltpu.VMEM)
ANY = pl.BlockSpec(memory_space=pl.ANY)
SMEM = pl.BlockSpec(memory_space=pltpu.SMEM)
WHOLE = pltpu.CompilerParams(vmem_limit_bytes=63 * 2**20)
PARAMS = pltpu.CompilerParams(vmem_limit_bytes=40 * 2**20)


def on_device(queries, seq_keys, seq_values, memory_keys, memory_values, retrieval, fifo_head, head_gate, norm_gain):
    me = lax.axis_index("seq")
    pos = jnp.stack([me // NZ, (me % NZ) // 2, me % 2]).astype(jnp.int32)
    flat = lambda a: a.reshape(2 * TOK, DH)
    q_parts = pl.pallas_call(
        query_kernel,
        out_shape=jax.ShapeDtypeStruct((NC, QROWS, DH), jnp.bfloat16),
        in_specs=[ANY] * 3,
        out_specs=VMEM,
        scratch_shapes=[
            pltpu.SMEM((1, 8), jnp.int32),
            pltpu.SMEM((1,), jnp.int32),
            pltpu.VMEM((2 * TOK, DH), jnp.bfloat16),
            pltpu.SemaphoreType.DMA((3,)),
        ],
        compiler_params=WHOLE,
        name="query",
    )(retrieval, fifo_head, flat(queries))
    q_all = lax.all_to_all(q_parts, "seq", 0, 0, axis_index_groups=C_GROUPS, tiled=True)
    kv = pl.pallas_call(
        code_kernel,
        out_shape=jax.ShapeDtypeStruct((KVROWS, DH), jnp.int16),
        in_specs=[ANY] * 4,
        out_specs=VMEM,
        scratch_shapes=[
            pltpu.VMEM((4, 2 * TOK, DH), jnp.bfloat16),
            pltpu.SemaphoreType.DMA((4,)),
        ],
        compiler_params=WHOLE,
        name="code",
    )(*map(flat, (seq_keys, seq_values, memory_keys, memory_values)))
    kv_all = lax.all_gather(kv, "seq", axis_index_groups=R_GROUPS)
    parts = pl.pallas_call(
        attend_kernel,
        out_shape=jax.ShapeDtypeStruct((NC, OROWS, DH), jnp.bfloat16),
        in_specs=[SMEM, VMEM, VMEM],
        out_specs=VMEM,
        scratch_shapes=SCRATCH,
        compiler_params=PARAMS,
        name="attend",
    )(pos, q_all, kv_all)
    parts = lax.all_to_all(parts, "seq", 0, 0, axis_index_groups=C_GROUPS, tiled=True)
    gate = jnp.broadcast_to(jax.nn.sigmoid(head_gate)[:, None], (2, TOK))
    comb, squares = pl.pallas_call(
        merge_kernel,
        out_shape=(
            jax.ShapeDtypeStruct((2, DH, TOK), jnp.float32),
            jax.ShapeDtypeStruct((8, TOK), jnp.float32),
        ),
        in_specs=[VMEM, VMEM],
        out_specs=(VMEM, VMEM),
        compiler_params=PARAMS,
        name="merge",
    )(gate, parts)
    squares = lax.all_to_all(squares, "head", 0, 0, tiled=True)
    out = pl.pallas_call(
        final_kernel,
        out_shape=jax.ShapeDtypeStruct((2 * TOK, DH), jnp.bfloat16),
        in_specs=[VMEM] * 3,
        out_specs=VMEM,
        compiler_params=PARAMS,
        name="final",
    )(squares, comb, norm_gain)
    return out.reshape(TOK, 2, DH)


def solution(mesh):
    in_specs = (P("seq", "head", None),) * 5 + (P("seq", None), P(), P("head"), P("head", None))
    return jax.shard_map(
        on_device, mesh=mesh, in_specs=in_specs, out_specs=P("seq", "head", None), check_vma=False
    )
```

```python
import jax
import jax.numpy as jnp
from jax import lax
from jax.experimental import pallas as pl
from jax.experimental.pallas import tpu as pltpu
from jax.sharding import PartitionSpec as P

HEADS = 16
DH = 128
TOK = 128
EXPIRED = 4
BLOCKS = 64
NX, NZ = 4, 16
NR = 8
NC = 8
QROWS = 2 * TOK + 16
OROWS = 4 * DH + 16
KVROWS = 8 * TOK + 16
NEG = -1e30
FLOOR = -1e29
LOG2_SCALE = DH**-0.5 * 1.4426950408889634

R_GROUPS = [[x * NZ + 2 * r + par for r in range(NR)] for x in range(NX) for par in range(2)]
NH = 8
C_GROUPS = [
    [(x * NZ + (2 * k + par + head % 2) % NZ) * NH + head for x in range(NX) for par in range(2)]
    for head in range(NH)
    for k in range(NZ // 2)
]

NT = (((1,), (1,)), ((), ()))
NN = (((1,), (0,)), ((), ()))


def dot(a, b, dims):
    return lax.dot_general(a, b, dims, preferred_element_type=jnp.float32)


def split_perm():
    row = lax.broadcasted_iota(jnp.int32, (2 * TOK, 2 * TOK), 0)
    col = lax.broadcasted_iota(jnp.int32, (2 * TOK, 2 * TOK), 1)
    source = (row % TOK) * 2 + row // TOK
    return jnp.where(col == source, 1.0, 0.0).astype(jnp.bfloat16)


def query_kernel(want_hbm, fifo_hbm, q_hbm, q_out, want, fifo, q_in, sems):
    core = lax.axis_index("head") % 2
    copies = [
        pltpu.make_async_copy(src, dst, sems.at[i])
        for i, (src, dst) in enumerate(((want_hbm, want), (fifo_hbm, fifo), (q_hbm, q_in)))
    ]
    for copy in copies:
        copy.start()
    perm = split_perm()
    for copy in copies:
        copy.wait()
    q_rows = dot(perm, q_in[...], NN).astype(jnp.bfloat16)
    row = lax.broadcasted_iota(jnp.int32, (16, TOK), 0)
    for c in range(NC):
        q_out[c, pl.ds(0, 2 * TOK), :] = q_rows
        block = (c // 2) * NZ + 2 * row + (c + core) % 2
        chosen = block == want[0, 0]
        for i in range(1, 8):
            chosen = chosen | (block == want[0, i])
        live = ((block - fifo[0] + BLOCKS) & (BLOCKS - 1)) >= EXPIRED
        q_out[c, pl.ds(2 * TOK, 16), :] = jnp.where(chosen & live, 0.0, NEG).astype(jnp.bfloat16)


def code_kernel(k_hbm, v_hbm, mk_hbm, mv_hbm, kv_out, rows_in, sems):
    copies = [
        pltpu.make_async_copy(src, rows_in.at[i], sems.at[i])
        for i, src in enumerate((k_hbm, v_hbm, mk_hbm, mv_hbm))
    ]
    for copy in copies:
        copy.start()
    perm = split_perm()
    powers = []
    for i, copy in enumerate(copies):
        copy.wait()
        rows = dot(perm, rows_in[i], NN)
        for h in range(2):
            block = rows[h * TOK : (h + 1) * TOK, :]
            if i % 2:
                block = jnp.transpose(block)
            peak = jnp.max(jnp.max(jnp.abs(block), 0, keepdims=True), 1, keepdims=True)
            power = jnp.floor(14.999 - jnp.log2(jnp.maximum(peak, 1e-30)))
            power = jnp.broadcast_to(power, (1, TOK))
            code = jnp.floor(block * jnp.exp2(power) + 0.5).astype(jnp.int32)
            kv_out[pl.ds((i * 2 + h) * TOK, TOK), :] = code.astype(jnp.int16)
            powers.append(power)
    powers.append(jnp.zeros((8, TOK), jnp.float32))
    tile = jnp.concatenate(powers, 0).astype(jnp.int32)
    kv_out[pl.ds(8 * TOK, 16), :] = tile.astype(jnp.int16)


def tok_start(r):
    return r * TOK if isinstance(r, int) else pl.multiple_of(r * TOK, TOK)


def decode(kv_ref, keys_ref, vals_ref):
    for r in range(NR):
        power = kv_ref[r, pl.ds(8 * TOK, 16), :].astype(jnp.int32).astype(jnp.float32)
        factor = jnp.exp2(-power)
        for i in range(4):
            for h in range(2):
                code = kv_ref[r, pl.ds((i * 2 + h) * TOK, TOK), :].astype(jnp.bfloat16)
                block = code * factor[i * 2 + h : i * 2 + h + 1, :].astype(jnp.bfloat16)
                at = (i // 2) * 2 + h
                if i % 2:
                    vals_ref[at, :, pl.ds(r * TOK, TOK)] = block
                else:
                    keys_ref[at, pl.ds(r * TOK, TOK), :] = block


def attend_kernel(
    pos_ref, q_ref, kv_ref, out_ref, keys_ref, vals_ref, s_ref, bias_ref, stat_ref, slot_ref
):
    decode(kv_ref, keys_ref, vals_ref)
    my_x, my_par, first_z = pos_ref[0], pos_ref[1], pos_ref[2]
    lane = lax.broadcasted_iota(jnp.int32, (TOK, 2 * TOK), 1)
    ahead = lax.broadcasted_iota(jnp.int32, (TOK, 2 * TOK), 0) - lane
    ahead = ahead + jnp.where((lane >= TOK) & (first_z == NZ - 1), NZ * TOK, 0)
    row = lax.broadcasted_iota(jnp.int32, (16, TOK), 0)
    place = jnp.where(row < NR, jnp.left_shift(1, row), 0).astype(jnp.float32)

    def run(xq, kind, blocks, mask):
        tops = []
        for h in range(2):
            at = kind * 2 + h
            q_rows = jnp.concatenate(
                [q_ref[2 * xq + par, pl.ds(h * TOK, TOK), :] for par in range(2)], 0
            )
            top = jnp.full((8, 2 * TOK), FLOOR, jnp.float32)
            for i, r in enumerate(blocks):
                s = mask(i, dot(keys_ref[at, pl.ds(tok_start(r), TOK), :], q_rows, NT))
                s_ref[at, pl.ds(i * TOK, TOK), :] = s
                top = jnp.maximum(top, jnp.max(s.reshape(TOK // 8, 8, 2 * TOK), 0))
            tops.append(jnp.max(top, 0, keepdims=True) * LOG2_SCALE)
        for h in range(2):
            at = kind * 2 + h
            top = tops[h]
            total = jnp.zeros((8, 2 * TOK), jnp.float32)
            acc = jnp.zeros((DH, 2 * TOK), jnp.float32)
            for i in range(0, len(blocks), 2):
                e = jnp.exp2(s_ref[at, pl.ds(i * TOK, 2 * TOK), :] * LOG2_SCALE - top)
                total = total + jnp.sum(e.reshape(2 * TOK // 8, 8, 2 * TOK), 0)
                vals = jnp.concatenate(
                    [vals_ref[at, :, pl.ds(tok_start(r), TOK)] for r in blocks[i : i + 2]], 1
                )
                acc = acc + dot(vals, e.astype(jnp.bfloat16), NN)
            total = jnp.maximum(jnp.sum(total, 0, keepdims=True), 1e-30)
            acc = (acc * (1.0 / total)).astype(jnp.bfloat16)
            for par in range(2):
                out_ref[2 * xq + par, pl.ds(at * DH, DH), :] = acc[:, par * TOK : (par + 1) * TOK]
            lse = top + jnp.log2(total)
            for i in range(3):
                part = lse.astype(jnp.bfloat16).astype(jnp.float32)
                stat_ref[at * 3 + i : at * 3 + i + 1, :] = part
                lse = lse - part

    def step(xq, carry):
        def causal(r, s):
            gap = ((xq - my_x) * NZ + first_z - 2 * r - my_par) * TOK
            return jnp.where(ahead <= gap, s, NEG)

        extra = [q_ref[2 * xq + par, pl.ds(2 * TOK, 16), :].astype(jnp.float32) for par in range(2)]
        bias_ref[...] = jnp.concatenate(extra, 1)
        wanted = jnp.where(jnp.maximum(extra[0], extra[1]) > -1.0, place, 0.0)
        bits = jnp.max(jnp.sum(wanted, 0, keepdims=True)).astype(jnp.int32)
        for r in range(NR):
            slot_ref[r] = 0
        count = jnp.int32(0)
        for r in range(NR):
            slot_ref[count] = r
            count = count + (jnp.right_shift(bits, r) & 1)

        run(xq, 0, list(range(NR)), causal)

        def some(size):
            blocks = [slot_ref[i] for i in range(size)]

            def retrieved(i, s):
                return s + jnp.where(i < count, bias_ref[pl.ds(blocks[i], 1), :], NEG)

            run(xq, 1, blocks, retrieved)

        @pl.when(count <= 2)
        def _():
            some(2)

        @pl.when((count > 2) & (count <= 4))
        def _():
            some(4)

        @pl.when(count > 4)
        def _():
            some(8)

        tile = stat_ref[...].astype(jnp.bfloat16)
        for par in range(2):
            out_ref[2 * xq + par, pl.ds(4 * DH, 16), :] = tile[:, par * TOK : (par + 1) * TOK]
        return carry

    stat_ref[...] = jnp.zeros((16, 2 * TOK), jnp.float32)
    lax.fori_loop(0, NX, step, 0)


SCRATCH = [
    pltpu.VMEM((4, NR * TOK, DH), jnp.bfloat16),
    pltpu.VMEM((4, DH, NR * TOK), jnp.bfloat16),
    pltpu.VMEM((4, NR * TOK, 2 * TOK), jnp.float32),
    pltpu.VMEM((16, 2 * TOK), jnp.float32),
    pltpu.VMEM((16, 2 * TOK), jnp.float32),
    pltpu.SMEM((8,), jnp.int32),
]


def merge_kernel(gate_ref, part_ref, comb_ref, sq_ref):
    stats = [part_ref[c, pl.ds(4 * DH, 16), :].astype(jnp.float32) for c in range(NC)]
    squares = jnp.zeros((1, TOK), jnp.float32)
    for h in range(2):
        merged = []
        for kind in range(2):
            at = (kind * 2 + h) * 3
            lse = [st[at : at + 1] + st[at + 1 : at + 2] + st[at + 2 : at + 3] for st in stats]
            top = lse[0]
            for one in lse[1:]:
                top = jnp.maximum(top, one)
            weight = [jnp.exp2(one - top) for one in lse]
            total = weight[0]
            for one in weight[1:]:
                total = total + one
            acc = jnp.zeros((DH, TOK), jnp.float32)
            for c in range(NC):
                rows = part_ref[c, pl.ds((kind * 2 + h) * DH, DH), :].astype(jnp.float32)
                acc = acc + rows * weight[c]
            merged.append(acc * (1.0 / total))
        gate = gate_ref[h : h + 1, :]
        comb = gate * merged[1] + (1.0 - gate) * merged[0]
        comb_ref[h] = comb
        squares = squares + jnp.sum(comb * comb, 0, keepdims=True)
    sq_ref[...] = jnp.broadcast_to(squares, (8, TOK))


def final_kernel(sq_ref, comb_ref, gain_ref, out_ref):
    mean_square = jnp.sum(sq_ref[...], 0, keepdims=True) * (1.0 / (HEADS * DH))
    scale = lax.rsqrt(mean_square + 1e-06)
    diag = lax.broadcasted_iota(jnp.int32, (DH, DH), 0) == lax.broadcasted_iota(jnp.int32, (DH, DH), 1)
    cols = []
    for h in range(2):
        gain = jnp.sum(jnp.where(diag, gain_ref[h : h + 1, :], 0.0), 1, keepdims=True)
        cols.append((comb_ref[h] * scale * gain).astype(jnp.bfloat16))
    row = lax.broadcasted_iota(jnp.int32, (2 * TOK, 2 * TOK), 0)
    col = lax.broadcasted_iota(jnp.int32, (2 * TOK, 2 * TOK), 1)
    pick = jnp.where(col == (row % 2) * TOK + row // 2, 1.0, 0.0).astype(jnp.bfloat16)
    out_ref[...] = dot(pick, jnp.concatenate(cols, 1), NT).astype(jnp.bfloat16)


VMEM = pl.BlockSpec(memory_space=pltpu.VMEM)
ANY = pl.BlockSpec(memory_space=pl.ANY)
SMEM = pl.BlockSpec(memory_space=pltpu.SMEM)
WHOLE = pltpu.CompilerParams(vmem_limit_bytes=63 * 2**20)
PARAMS = pltpu.CompilerParams(vmem_limit_bytes=40 * 2**20)


def on_device(queries, seq_keys, seq_values, memory_keys, memory_values, retrieval, fifo_head, head_gate, norm_gain):
    me = lax.axis_index("seq")
    core = lax.axis_index("head") % 2
    first_z = (me - core + NZ) % NZ // 2 * 2 + core
    pos = jnp.stack([me // NZ, me % 2, first_z]).astype(jnp.int32)
    flat = lambda a: a.reshape(2 * TOK, DH)
    q_parts = pl.pallas_call(
        query_kernel,
        out_shape=jax.ShapeDtypeStruct((NC, QROWS, DH), jnp.bfloat16),
        in_specs=[ANY] * 3,
        out_specs=VMEM,
        scratch_shapes=[
            pltpu.SMEM((1, 8), jnp.int32),
            pltpu.SMEM((1,), jnp.int32),
            pltpu.VMEM((2 * TOK, DH), jnp.bfloat16),
            pltpu.SemaphoreType.DMA((3,)),
        ],
        compiler_params=WHOLE,
        name="query",
    )(retrieval, fifo_head, flat(queries))
    q_all = lax.all_to_all(q_parts, ("seq", "head"), 0, 0, axis_index_groups=C_GROUPS, tiled=True)
    kv = pl.pallas_call(
        code_kernel,
        out_shape=jax.ShapeDtypeStruct((KVROWS, DH), jnp.int16),
        in_specs=[ANY] * 4,
        out_specs=VMEM,
        scratch_shapes=[
            pltpu.VMEM((4, 2 * TOK, DH), jnp.bfloat16),
            pltpu.SemaphoreType.DMA((4,)),
        ],
        compiler_params=PARAMS,
        name="code",
    )(*map(flat, (seq_keys, seq_values, memory_keys, memory_values)))
    kv_all = lax.all_gather(kv, "seq", axis_index_groups=R_GROUPS)
    parts = pl.pallas_call(
        attend_kernel,
        out_shape=jax.ShapeDtypeStruct((NC, OROWS, DH), jnp.bfloat16),
        in_specs=[SMEM, VMEM, VMEM],
        out_specs=VMEM,
        scratch_shapes=SCRATCH,
        compiler_params=PARAMS,
        name="attend",
    )(pos, q_all, kv_all)
    parts = lax.all_to_all(parts, ("seq", "head"), 0, 0, axis_index_groups=C_GROUPS, tiled=True)
    gate = jnp.broadcast_to(jax.nn.sigmoid(head_gate)[:, None], (2, TOK))
    comb, squares = pl.pallas_call(
        merge_kernel,
        out_shape=(
            jax.ShapeDtypeStruct((2, DH, TOK), jnp.float32),
            jax.ShapeDtypeStruct((8, TOK), jnp.float32),
        ),
        in_specs=[VMEM, VMEM],
        out_specs=(VMEM, VMEM),
        compiler_params=PARAMS,
        name="merge",
    )(gate, parts)
    squares = lax.all_to_all(squares, "head", 0, 0, tiled=True)
    out = pl.pallas_call(
        final_kernel,
        out_shape=jax.ShapeDtypeStruct((2 * TOK, DH), jnp.bfloat16),
        in_specs=[VMEM] * 3,
        out_specs=VMEM,
        compiler_params=PARAMS,
        name="final",
    )(squares, comb, norm_gain)
    return out.reshape(TOK, 2, DH)


def solution(mesh):
    in_specs = (P("seq", "head", None),) * 5 + (P("seq", None), P(), P("head"), P("head", None))
    return jax.shard_map(
        on_device, mesh=mesh, in_specs=in_specs, out_specs=P("seq", "head", None), check_vma=False
    )
```

```python
import jax
import jax.numpy as jnp
from jax import lax
from jax.experimental import pallas as pl
from jax.experimental.pallas import tpu as pltpu
from jax.sharding import PartitionSpec as P

HEADS = 16
DH = 128
TOK = 128
EXPIRED = 4
BLOCKS = 64
NX, NZ = 4, 16
NR = 8
NC = 8
QROWS = 2 * TOK + 16
OROWS = 4 * DH + 16
KVROWS = 8 * TOK + 16
NEG = -1e30
FLOOR = -1e29
LOG2_SCALE = DH**-0.5 * 1.4426950408889634

R_GROUPS = [[x * NZ + 2 * r + par for r in range(NR)] for x in range(NX) for par in range(2)]
C_GROUPS = [[x * NZ + 2 * k + par for x in range(NX) for par in range(2)] for k in range(NZ // 2)]

NT = (((1,), (1,)), ((), ()))
NN = (((1,), (0,)), ((), ()))


def dot(a, b, dims):
    return lax.dot_general(a, b, dims, preferred_element_type=jnp.float32)


def split_perm():
    row = lax.broadcasted_iota(jnp.int32, (2 * TOK, 2 * TOK), 0)
    col = lax.broadcasted_iota(jnp.int32, (2 * TOK, 2 * TOK), 1)
    source = (row % TOK) * 2 + row // TOK
    return jnp.where(col == source, 1.0, 0.0).astype(jnp.bfloat16)


def query_kernel(want_hbm, fifo_hbm, q_hbm, q_out, want, fifo, q_in, sems):
    copies = [
        pltpu.make_async_copy(src, dst, sems.at[i])
        for i, (src, dst) in enumerate(((want_hbm, want), (fifo_hbm, fifo), (q_hbm, q_in)))
    ]
    for copy in copies:
        copy.start()
    perm = split_perm()
    row = lax.broadcasted_iota(jnp.int32, (16, TOK), 0)
    copies[0].wait()
    copies[1].wait()
    for c in range(NC):
        block = (c // 2) * NZ + 2 * row + c % 2
        chosen = block == want[0, 0]
        for i in range(1, 8):
            chosen = chosen | (block == want[0, i])
        live = ((block - fifo[0] + BLOCKS) & (BLOCKS - 1)) >= EXPIRED
        q_out[c, pl.ds(2 * TOK, 16), :] = jnp.where(chosen & live, 0.0, NEG).astype(jnp.bfloat16)
    copies[2].wait()
    q_rows = dot(perm, q_in[...], NN).astype(jnp.bfloat16)
    for c in range(NC):
        q_out[c, pl.ds(0, 2 * TOK), :] = q_rows


def code_kernel(k_hbm, v_hbm, mk_hbm, mv_hbm, kv_out, rows_in, sems):
    copies = [
        pltpu.make_async_copy(src, rows_in.at[i], sems.at[i])
        for i, src in enumerate((k_hbm, v_hbm, mk_hbm, mv_hbm))
    ]
    for copy in copies:
        copy.start()
    perm = split_perm()
    powers = []
    for i, copy in enumerate(copies):
        copy.wait()
        rows = dot(perm, rows_in[i], NN)
        for h in range(2):
            block = rows[h * TOK : (h + 1) * TOK, :]
            if i % 2:
                block = jnp.transpose(block)
            peak = jnp.max(jnp.max(jnp.abs(block), 0, keepdims=True), 1, keepdims=True)
            power = jnp.floor(14.999 - jnp.log2(jnp.maximum(peak, 1e-30)))
            power = jnp.broadcast_to(power, (1, TOK))
            code = jnp.floor(block * jnp.exp2(power) + 0.5).astype(jnp.int32)
            kv_out[pl.ds((i * 2 + h) * TOK, TOK), :] = code.astype(jnp.int16)
            powers.append(power)
    powers.append(jnp.zeros((8, TOK), jnp.float32))
    tile = jnp.concatenate(powers, 0).astype(jnp.int32)
    kv_out[pl.ds(8 * TOK, 16), :] = tile.astype(jnp.int16)


def tok_start(r):
    return r * TOK if isinstance(r, int) else pl.multiple_of(r * TOK, TOK)


def decode(kv_ref, keys_ref, vals_ref):
    for r in range(NR):
        power = kv_ref[r, pl.ds(8 * TOK, 16), :].astype(jnp.int32).astype(jnp.float32)
        factor = jnp.exp2(-power)
        for i in range(4):
            for h in range(2):
                code = kv_ref[r, pl.ds((i * 2 + h) * TOK, TOK), :].astype(jnp.bfloat16)
                block = code * factor[i * 2 + h : i * 2 + h + 1, :].astype(jnp.bfloat16)
                at = (i // 2) * 2 + h
                if i % 2:
                    vals_ref[at, pl.ds(0, DH), pl.ds(r * TOK, TOK)] = block
                else:
                    keys_ref[at, pl.ds(r * TOK, TOK), :] = block


def attend_kernel(
    pos_ref, q_ref, kv_ref, out_ref, keys_ref, vals_ref, s_ref, bias_ref, stat_ref, slot_ref
):
    decode(kv_ref, keys_ref, vals_ref)
    for at in range(4):
        vals_ref[at, pl.ds(DH, 16), :] = jnp.ones((16, NR * TOK), jnp.bfloat16)
    my_x, my_pair, my_par = pos_ref[0], pos_ref[1], pos_ref[2]
    ahead = lax.broadcasted_iota(jnp.int32, (TOK, 2 * TOK), 0) - lax.broadcasted_iota(
        jnp.int32, (TOK, 2 * TOK), 1
    )
    row = lax.broadcasted_iota(jnp.int32, (16, TOK), 0)
    place = jnp.where(row < NR, jnp.left_shift(1, row), 0).astype(jnp.float32)

    def run(xq, kind, blocks, mask):
        tops = []
        for h in range(2):
            at = kind * 2 + h
            q_rows = jnp.concatenate(
                [q_ref[2 * xq + par, pl.ds(h * TOK, TOK), :] for par in range(2)], 0
            )
            top = jnp.full((8, 2 * TOK), FLOOR, jnp.float32)
            for i, r in enumerate(blocks):
                s = mask(i, dot(keys_ref[at, pl.ds(tok_start(r), TOK), :], q_rows, NT))
                s_ref[at, pl.ds(i * TOK, TOK), :] = s
                top = jnp.maximum(top, jnp.max(s.reshape(TOK // 8, 8, 2 * TOK), 0))
            tops.append(jnp.max(top, 0, keepdims=True) * LOG2_SCALE)
        for h in range(2):
            at = kind * 2 + h
            top = tops[h]
            acc = jnp.zeros((DH + 16, 2 * TOK), jnp.float32)
            for i in range(0, len(blocks), 2):
                part = blocks[i : i + 2]
                e = jnp.exp2(s_ref[at, pl.ds(i * TOK, len(part) * TOK), :] * LOG2_SCALE - top)
                vals = jnp.concatenate([vals_ref[at, :, pl.ds(tok_start(r), TOK)] for r in part], 1)
                acc = acc + dot(vals, e.astype(jnp.bfloat16), NN)
            total = jnp.maximum(acc[DH : DH + 1, :], 1e-30)
            acc = (acc[:DH, :] * (1.0 / total)).astype(jnp.bfloat16)
            for par in range(2):
                out_ref[2 * xq + par, pl.ds(at * DH, DH), :] = acc[:, par * TOK : (par + 1) * TOK]
            lse = top + jnp.log2(total)
            for i in range(3):
                part = lse.astype(jnp.bfloat16).astype(jnp.float32)
                stat_ref[at * 3 + i : at * 3 + i + 1, :] = part
                lse = lse - part

    def step(xq, carry):
        def causal(r, s):
            gap = ((xq - my_x) * NZ + 2 * my_pair - 2 * r - my_par) * TOK
            return jnp.where(ahead <= gap, s, NEG)

        extra = [q_ref[2 * xq + par, pl.ds(2 * TOK, 16), :].astype(jnp.float32) for par in range(2)]
        bias_ref[...] = jnp.concatenate(extra, 1)
        wanted = jnp.where(jnp.maximum(extra[0], extra[1]) > -1.0, place, 0.0)
        bits = jnp.max(jnp.sum(wanted, 0, keepdims=True)).astype(jnp.int32)
        for r in range(NR):
            slot_ref[r] = 0
        count = jnp.int32(0)
        for r in range(NR):
            slot_ref[count] = r
            count = count + (jnp.right_shift(bits, r) & 1)

        run(xq, 0, list(range(NR)), causal)

        def some(size):
            blocks = [slot_ref[i] for i in range(size)]

            def retrieved(i, s):
                return s + jnp.where(i < count, bias_ref[pl.ds(blocks[i], 1), :], NEG)

            run(xq, 1, blocks, retrieved)

        @pl.when(count <= 2)
        def _():
            some(2)

        @pl.when((count > 2) & (count <= 4))
        def _():
            some(4)

        @pl.when(count > 4)
        def _():
            some(8)

        tile = stat_ref[...].astype(jnp.bfloat16)
        for par in range(2):
            out_ref[2 * xq + par, pl.ds(4 * DH, 16), :] = tile[:, par * TOK : (par + 1) * TOK]
        return carry

    stat_ref[...] = jnp.zeros((16, 2 * TOK), jnp.float32)
    lax.fori_loop(0, NX, step, 0)


SCRATCH = [
    pltpu.VMEM((4, NR * TOK, DH), jnp.bfloat16),
    pltpu.VMEM((4, DH + 16, NR * TOK), jnp.bfloat16),
    pltpu.VMEM((4, NR * TOK, 2 * TOK), jnp.float32),
    pltpu.VMEM((16, 2 * TOK), jnp.float32),
    pltpu.VMEM((16, 2 * TOK), jnp.float32),
    pltpu.SMEM((8,), jnp.int32),
]


def merge_kernel(gate_ref, part_ref, comb_ref, sq_ref):
    stats = [part_ref[c, pl.ds(4 * DH, 16), :].astype(jnp.float32) for c in range(NC)]
    squares = jnp.zeros((1, TOK), jnp.float32)
    for h in range(2):
        merged = []
        for kind in range(2):
            at = (kind * 2 + h) * 3
            lse = [st[at : at + 1] + st[at + 1 : at + 2] + st[at + 2 : at + 3] for st in stats]
            top = lse[0]
            for one in lse[1:]:
                top = jnp.maximum(top, one)
            weight = [jnp.exp2(one - top) for one in lse]
            total = weight[0]
            for one in weight[1:]:
                total = total + one
            acc = jnp.zeros((DH, TOK), jnp.float32)
            for c in range(NC):
                rows = part_ref[c, pl.ds((kind * 2 + h) * DH, DH), :].astype(jnp.float32)
                acc = acc + rows * weight[c]
            merged.append(acc * (1.0 / total))
        gate = gate_ref[h : h + 1, :]
        comb = gate * merged[1] + (1.0 - gate) * merged[0]
        comb_ref[h] = comb
        squares = squares + jnp.sum(comb * comb, 0, keepdims=True)
    sq_ref[...] = jnp.broadcast_to(squares, (8, TOK))


def final_kernel(sq_ref, comb_ref, gain_ref, out_ref):
    mean_square = jnp.sum(sq_ref[...], 0, keepdims=True) * (1.0 / (HEADS * DH))
    scale = lax.rsqrt(mean_square + 1e-06)
    diag = lax.broadcasted_iota(jnp.int32, (DH, DH), 0) == lax.broadcasted_iota(jnp.int32, (DH, DH), 1)
    cols = []
    for h in range(2):
        gain = jnp.sum(jnp.where(diag, gain_ref[h : h + 1, :], 0.0), 1, keepdims=True)
        cols.append((comb_ref[h] * scale * gain).astype(jnp.bfloat16))
    row = lax.broadcasted_iota(jnp.int32, (2 * TOK, 2 * TOK), 0)
    col = lax.broadcasted_iota(jnp.int32, (2 * TOK, 2 * TOK), 1)
    pick = jnp.where(col == (row % 2) * TOK + row // 2, 1.0, 0.0).astype(jnp.bfloat16)
    out_ref[...] = dot(pick, jnp.concatenate(cols, 1), NT).astype(jnp.bfloat16)


VMEM = pl.BlockSpec(memory_space=pltpu.VMEM)
ANY = pl.BlockSpec(memory_space=pl.ANY)
SMEM = pl.BlockSpec(memory_space=pltpu.SMEM)
WHOLE = pltpu.CompilerParams(vmem_limit_bytes=63 * 2**20)
PARAMS = pltpu.CompilerParams(vmem_limit_bytes=40 * 2**20)


def on_device(queries, seq_keys, seq_values, memory_keys, memory_values, retrieval, fifo_head, head_gate, norm_gain):
    me = lax.axis_index("seq")
    pos = jnp.stack([me // NZ, (me % NZ) // 2, me % 2]).astype(jnp.int32)
    flat = lambda a: a.reshape(2 * TOK, DH)
    q_parts = pl.pallas_call(
        query_kernel,
        out_shape=jax.ShapeDtypeStruct((NC, QROWS, DH), jnp.bfloat16),
        in_specs=[ANY] * 3,
        out_specs=VMEM,
        scratch_shapes=[
            pltpu.SMEM((1, 8), jnp.int32),
            pltpu.SMEM((1,), jnp.int32),
            pltpu.VMEM((2 * TOK, DH), jnp.bfloat16),
            pltpu.SemaphoreType.DMA((3,)),
        ],
        compiler_params=WHOLE,
        name="query",
    )(retrieval, fifo_head, flat(queries))
    q_all = lax.all_to_all(q_parts, "seq", 0, 0, axis_index_groups=C_GROUPS, tiled=True)
    kv = pl.pallas_call(
        code_kernel,
        out_shape=jax.ShapeDtypeStruct((KVROWS, DH), jnp.int16),
        in_specs=[ANY] * 4,
        out_specs=VMEM,
        scratch_shapes=[
            pltpu.VMEM((4, 2 * TOK, DH), jnp.bfloat16),
            pltpu.SemaphoreType.DMA((4,)),
        ],
        compiler_params=PARAMS,
        name="code",
    )(*map(flat, (seq_keys, seq_values, memory_keys, memory_values)))
    kv_all = lax.all_gather(kv, "seq", axis_index_groups=R_GROUPS)
    parts = pl.pallas_call(
        attend_kernel,
        out_shape=jax.ShapeDtypeStruct((NC, OROWS, DH), jnp.bfloat16),
        in_specs=[SMEM, VMEM, VMEM],
        out_specs=VMEM,
        scratch_shapes=SCRATCH,
        compiler_params=PARAMS,
        name="attend",
    )(pos, q_all, kv_all)
    parts = lax.all_to_all(parts, "seq", 0, 0, axis_index_groups=C_GROUPS, tiled=True)
    gate = jnp.broadcast_to(jax.nn.sigmoid(head_gate)[:, None], (2, TOK))
    comb, squares = pl.pallas_call(
        merge_kernel,
        out_shape=(
            jax.ShapeDtypeStruct((2, DH, TOK), jnp.float32),
            jax.ShapeDtypeStruct((8, TOK), jnp.float32),
        ),
        in_specs=[VMEM, VMEM],
        out_specs=(VMEM, VMEM),
        compiler_params=PARAMS,
        name="merge",
    )(gate, parts)
    squares = lax.all_to_all(squares, "head", 0, 0, tiled=True)
    out = pl.pallas_call(
        final_kernel,
        out_shape=jax.ShapeDtypeStruct((2 * TOK, DH), jnp.bfloat16),
        in_specs=[VMEM] * 3,
        out_specs=VMEM,
        compiler_params=PARAMS,
        name="final",
    )(squares, comb, norm_gain)
    return out.reshape(TOK, 2, DH)


def solution(mesh):
    in_specs = (P("seq", "head", None),) * 5 + (P("seq", None), P(), P("head"), P("head", None))
    return jax.shard_map(
        on_device, mesh=mesh, in_specs=in_specs, out_specs=P("seq", "head", None), check_vma=False
    )
```

```python
import jax
import jax.numpy as jnp
from jax import lax
from jax.experimental import pallas as pl
from jax.experimental.pallas import tpu as pltpu
from jax.sharding import PartitionSpec as P

HEADS = 16
DH = 128
TOK = 128
EXPIRED = 4
BLOCKS = 64
NX, NZ = 4, 16
NR = 8
NC = 8
QROWS = 2 * TOK + 16
OROWS = 4 * DH + 16
KVROWS = 8 * TOK + 16
NEG = -1e30
FLOOR = -1e29
LOG2_SCALE = DH**-0.5 * 1.4426950408889634

R_GROUPS = [[x * NZ + 2 * r + par for r in range(NR)] for x in range(NX) for par in range(2)]
C_GROUPS = [[x * NZ + 2 * k + par for x in range(NX) for par in range(2)] for k in range(NZ // 2)]

NT = (((1,), (1,)), ((), ()))
NN = (((1,), (0,)), ((), ()))


def dot(a, b, dims):
    return lax.dot_general(a, b, dims, preferred_element_type=jnp.float32)


def split_perm():
    row = lax.broadcasted_iota(jnp.int32, (2 * TOK, 2 * TOK), 0)
    col = lax.broadcasted_iota(jnp.int32, (2 * TOK, 2 * TOK), 1)
    source = (row % TOK) * 2 + row // TOK
    return jnp.where(col == source, 1.0, 0.0).astype(jnp.bfloat16)


def query_kernel(want_hbm, fifo_hbm, q_hbm, q_out, want, fifo, q_in, sems):
    copies = [
        pltpu.make_async_copy(src, dst, sems.at[i])
        for i, (src, dst) in enumerate(((want_hbm, want), (fifo_hbm, fifo), (q_hbm, q_in)))
    ]
    for copy in copies:
        copy.start()
    perm = split_perm()
    row = lax.broadcasted_iota(jnp.int32, (16, TOK), 0)
    copies[0].wait()
    copies[1].wait()
    for c in range(NC):
        block = (c // 2) * NZ + 2 * row + c % 2
        chosen = block == want[0, 0]
        for i in range(1, 8):
            chosen = chosen | (block == want[0, i])
        live = ((block - fifo[0] + BLOCKS) & (BLOCKS - 1)) >= EXPIRED
        q_out[c, pl.ds(2 * TOK, 16), :] = jnp.where(chosen & live, 0.0, NEG).astype(jnp.bfloat16)
    copies[2].wait()
    q_rows = dot(perm, q_in[...], NN).astype(jnp.bfloat16)
    for c in range(NC):
        q_out[c, pl.ds(0, 2 * TOK), :] = q_rows


def code_kernel(k_hbm, v_hbm, mk_hbm, mv_hbm, kv_out, rows_in, sems):
    copies = [
        pltpu.make_async_copy(src, rows_in.at[i], sems.at[i])
        for i, src in enumerate((k_hbm, v_hbm, mk_hbm, mv_hbm))
    ]
    for copy in copies:
        copy.start()
    perm = split_perm()
    powers = []
    for i, copy in enumerate(copies):
        copy.wait()
        rows = dot(perm, rows_in[i], NN)
        for h in range(2):
            block = rows[h * TOK : (h + 1) * TOK, :]
            if i % 2:
                block = jnp.transpose(block)
            peak = jnp.max(jnp.max(jnp.abs(block), 0, keepdims=True), 1, keepdims=True)
            power = jnp.floor(14.997 - jnp.log2(jnp.maximum(peak, 1e-30)))
            power = jnp.broadcast_to(power, (1, TOK))
            code = jnp.floor(block * jnp.exp2(power) + 0.5)
            code = jnp.clip(code, -32767.0, 32767.0).astype(jnp.int32)
            kv_out[pl.ds((i * 2 + h) * TOK, TOK), :] = code.astype(jnp.int16)
            powers.append(power)
    powers.append(jnp.zeros((8, TOK), jnp.float32))
    tile = jnp.concatenate(powers, 0).astype(jnp.int32)
    kv_out[pl.ds(8 * TOK, 16), :] = tile.astype(jnp.int16)


def tok_start(r):
    return r * TOK if isinstance(r, int) else pl.multiple_of(r * TOK, TOK)


def decode(kv_ref, keys_ref, vals_ref):
    for r in range(NR):
        power = kv_ref[r, pl.ds(8 * TOK, 16), :].astype(jnp.int32).astype(jnp.float32)
        factor = jnp.exp2(-power)
        for i in range(4):
            for h in range(2):
                code = kv_ref[r, pl.ds((i * 2 + h) * TOK, TOK), :].astype(jnp.bfloat16)
                block = code * factor[i * 2 + h : i * 2 + h + 1, :].astype(jnp.bfloat16)
                at = (i // 2) * 2 + h
                if i % 2:
                    vals_ref[at, pl.ds(0, DH), pl.ds(r * TOK, TOK)] = block
                else:
                    keys_ref[at, pl.ds(r * TOK, TOK), :] = block


def attend_kernel(
    pos_ref, q_ref, kv_ref, out_ref, keys_ref, vals_ref, s_ref, bias_ref, stat_ref, slot_ref
):
    decode(kv_ref, keys_ref, vals_ref)
    for at in range(4):
        vals_ref[at, pl.ds(DH, 16), :] = jnp.ones((16, NR * TOK), jnp.bfloat16)
    my_x, my_pair, my_par = pos_ref[0], pos_ref[1], pos_ref[2]
    ahead = lax.broadcasted_iota(jnp.int32, (TOK, 2 * TOK), 0) - lax.broadcasted_iota(
        jnp.int32, (TOK, 2 * TOK), 1
    )
    row = lax.broadcasted_iota(jnp.int32, (16, TOK), 0)
    place = jnp.where(row < NR, jnp.left_shift(1, row), 0).astype(jnp.float32)

    def run(xq, kind, blocks, mask):
        tops = []
        for h in range(2):
            at = kind * 2 + h
            q_rows = jnp.concatenate(
                [q_ref[2 * xq + par, pl.ds(h * TOK, TOK), :] for par in range(2)], 0
            )
            top = jnp.full((8, 2 * TOK), FLOOR, jnp.float32)
            for i, r in enumerate(blocks):
                s = mask(i, dot(keys_ref[at, pl.ds(tok_start(r), TOK), :], q_rows, NT))
                s = s * LOG2_SCALE
                s_ref[at, pl.ds(i * TOK, TOK), :] = s
                top = jnp.maximum(top, jnp.max(s.reshape(TOK // 8, 8, 2 * TOK), 0))
            tops.append(jnp.max(top, 0, keepdims=True))
        for h in range(2):
            at = kind * 2 + h
            top = tops[h]
            acc = jnp.zeros((DH + 16, 2 * TOK), jnp.float32)
            for i in range(0, len(blocks), 2):
                part = blocks[i : i + 2]
                e = jnp.exp2(s_ref[at, pl.ds(i * TOK, len(part) * TOK), :] - top)
                vals = jnp.concatenate([vals_ref[at, :, pl.ds(tok_start(r), TOK)] for r in part], 1)
                acc = acc + dot(vals, e.astype(jnp.bfloat16), NN)
            total = jnp.maximum(acc[DH : DH + 1, :], 1e-30)
            acc = (acc[:DH, :] * (1.0 / total)).astype(jnp.bfloat16)
            for par in range(2):
                out_ref[2 * xq + par, pl.ds(at * DH, DH), :] = acc[:, par * TOK : (par + 1) * TOK]
            lse = top + jnp.log2(total)
            for i in range(3):
                part = lse.astype(jnp.bfloat16).astype(jnp.float32)
                stat_ref[at * 3 + i : at * 3 + i + 1, :] = part
                lse = lse - part

    def step(xq, carry):
        def causal(r, s):
            gap = ((xq - my_x) * NZ + 2 * my_pair - 2 * r - my_par) * TOK
            return jnp.where(ahead <= gap, s, NEG)

        extra = [q_ref[2 * xq + par, pl.ds(2 * TOK, 16), :].astype(jnp.float32) for par in range(2)]
        bias_ref[...] = jnp.concatenate(extra, 1)
        wanted = jnp.where(jnp.maximum(extra[0], extra[1]) > -1.0, place, 0.0)
        bits = jnp.max(jnp.sum(wanted, 0, keepdims=True)).astype(jnp.int32)
        for r in range(NR):
            slot_ref[r] = 0
        count = jnp.int32(0)
        for r in range(NR):
            slot_ref[count] = r
            count = count + (jnp.right_shift(bits, r) & 1)

        run(xq, 0, list(range(NR)), causal)

        def some(size):
            blocks = [slot_ref[i] for i in range(size)]

            def retrieved(i, s):
                return s + jnp.where(i < count, bias_ref[pl.ds(blocks[i], 1), :], NEG)

            run(xq, 1, blocks, retrieved)

        @pl.when(count <= 2)
        def _():
            some(2)

        @pl.when((count > 2) & (count <= 4))
        def _():
            some(4)

        @pl.when(count > 4)
        def _():
            some(8)

        tile = stat_ref[...].astype(jnp.bfloat16)
        for par in range(2):
            out_ref[2 * xq + par, pl.ds(4 * DH, 16), :] = tile[:, par * TOK : (par + 1) * TOK]
        return carry

    stat_ref[...] = jnp.zeros((16, 2 * TOK), jnp.float32)
    lax.fori_loop(0, NX, step, 0)


SCRATCH = [
    pltpu.VMEM((4, NR * TOK, DH), jnp.bfloat16),
    pltpu.VMEM((4, DH + 16, NR * TOK), jnp.bfloat16),
    pltpu.VMEM((4, NR * TOK, 2 * TOK), jnp.float32),
    pltpu.VMEM((16, 2 * TOK), jnp.float32),
    pltpu.VMEM((16, 2 * TOK), jnp.float32),
    pltpu.SMEM((8,), jnp.int32),
]


def merge_kernel(gate_ref, part_ref, comb_ref, sq_ref):
    stats = [part_ref[c, pl.ds(4 * DH, 16), :].astype(jnp.float32) for c in range(NC)]
    squares = jnp.zeros((1, TOK), jnp.float32)
    for h in range(2):
        merged = []
        for kind in range(2):
            at = (kind * 2 + h) * 3
            lse = [st[at : at + 1] + st[at + 1 : at + 2] + st[at + 2 : at + 3] for st in stats]
            top = lse[0]
            for one in lse[1:]:
                top = jnp.maximum(top, one)
            weight = [jnp.exp2(one - top) for one in lse]
            total = weight[0]
            for one in weight[1:]:
                total = total + one
            acc = jnp.zeros((DH, TOK), jnp.float32)
            for c in range(NC):
                rows = part_ref[c, pl.ds((kind * 2 + h) * DH, DH), :].astype(jnp.float32)
                acc = acc + rows * weight[c]
            merged.append(acc * (1.0 / total))
        gate = gate_ref[h : h + 1, :]
        comb = gate * merged[1] + (1.0 - gate) * merged[0]
        comb_ref[h] = comb
        squares = squares + jnp.sum(comb * comb, 0, keepdims=True)
    sq_ref[...] = jnp.broadcast_to(squares, (8, TOK))


def final_kernel(sq_ref, comb_ref, gain_ref, out_ref):
    mean_square = jnp.sum(sq_ref[...], 0, keepdims=True) * (1.0 / (HEADS * DH))
    scale = lax.rsqrt(mean_square + 1e-06)
    diag = lax.broadcasted_iota(jnp.int32, (DH, DH), 0) == lax.broadcasted_iota(jnp.int32, (DH, DH), 1)
    cols = []
    for h in range(2):
        gain = jnp.sum(jnp.where(diag, gain_ref[h : h + 1, :], 0.0), 1, keepdims=True)
        cols.append((comb_ref[h] * scale * gain).astype(jnp.bfloat16))
    row = lax.broadcasted_iota(jnp.int32, (2 * TOK, 2 * TOK), 0)
    col = lax.broadcasted_iota(jnp.int32, (2 * TOK, 2 * TOK), 1)
    pick = jnp.where(col == (row % 2) * TOK + row // 2, 1.0, 0.0).astype(jnp.bfloat16)
    out_ref[...] = dot(pick, jnp.concatenate(cols, 1), NT).astype(jnp.bfloat16)


VMEM = pl.BlockSpec(memory_space=pltpu.VMEM)
ANY = pl.BlockSpec(memory_space=pl.ANY)
SMEM = pl.BlockSpec(memory_space=pltpu.SMEM)
WHOLE = pltpu.CompilerParams(vmem_limit_bytes=63 * 2**20)
PARAMS = pltpu.CompilerParams(vmem_limit_bytes=40 * 2**20)


def on_device(queries, seq_keys, seq_values, memory_keys, memory_values, retrieval, fifo_head, head_gate, norm_gain):
    me = lax.axis_index("seq")
    pos = jnp.stack([me // NZ, (me % NZ) // 2, me % 2]).astype(jnp.int32)
    flat = lambda a: a.reshape(2 * TOK, DH)
    q_parts = pl.pallas_call(
        query_kernel,
        out_shape=jax.ShapeDtypeStruct((NC, QROWS, DH), jnp.bfloat16),
        in_specs=[ANY] * 3,
        out_specs=VMEM,
        scratch_shapes=[
            pltpu.SMEM((1, 8), jnp.int32),
            pltpu.SMEM((1,), jnp.int32),
            pltpu.VMEM((2 * TOK, DH), jnp.bfloat16),
            pltpu.SemaphoreType.DMA((3,)),
        ],
        compiler_params=WHOLE,
        name="query",
    )(retrieval, fifo_head, flat(queries))
    q_all = lax.all_to_all(q_parts, "seq", 0, 0, axis_index_groups=C_GROUPS, tiled=True)
    kv = pl.pallas_call(
        code_kernel,
        out_shape=jax.ShapeDtypeStruct((KVROWS, DH), jnp.int16),
        in_specs=[ANY] * 4,
        out_specs=VMEM,
        scratch_shapes=[
            pltpu.VMEM((4, 2 * TOK, DH), jnp.bfloat16),
            pltpu.SemaphoreType.DMA((4,)),
        ],
        compiler_params=PARAMS,
        name="code",
    )(*map(flat, (seq_keys, seq_values, memory_keys, memory_values)))
    kv_all = lax.all_gather(kv, "seq", axis_index_groups=R_GROUPS)
    parts = pl.pallas_call(
        attend_kernel,
        out_shape=jax.ShapeDtypeStruct((NC, OROWS, DH), jnp.bfloat16),
        in_specs=[SMEM, VMEM, VMEM],
        out_specs=VMEM,
        scratch_shapes=SCRATCH,
        compiler_params=PARAMS,
        name="attend",
    )(pos, q_all, kv_all)
    parts = lax.all_to_all(parts, "seq", 0, 0, axis_index_groups=C_GROUPS, tiled=True)
    gate = jnp.broadcast_to(jax.nn.sigmoid(head_gate)[:, None], (2, TOK))
    comb, squares = pl.pallas_call(
        merge_kernel,
        out_shape=(
            jax.ShapeDtypeStruct((2, DH, TOK), jnp.float32),
            jax.ShapeDtypeStruct((8, TOK), jnp.float32),
        ),
        in_specs=[VMEM, VMEM],
        out_specs=(VMEM, VMEM),
        compiler_params=PARAMS,
        name="merge",
    )(gate, parts)
    squares = lax.all_to_all(squares, "head", 0, 0, tiled=True)
    out = pl.pallas_call(
        final_kernel,
        out_shape=jax.ShapeDtypeStruct((2 * TOK, DH), jnp.bfloat16),
        in_specs=[VMEM] * 3,
        out_specs=VMEM,
        compiler_params=PARAMS,
        name="final",
    )(squares, comb, norm_gain)
    return out.reshape(TOK, 2, DH)


def solution(mesh):
    in_specs = (P("seq", "head", None),) * 5 + (P("seq", None), P(), P("head"), P("head", None))
    return jax.shard_map(
        on_device, mesh=mesh, in_specs=in_specs, out_specs=P("seq", "head", None), check_vma=False
    )
```

```python
import jax
import jax.numpy as jnp
from jax import lax
from jax.experimental import pallas as pl
from jax.experimental.pallas import tpu as pltpu
from jax.sharding import PartitionSpec as P

HEADS = 16
DH = 128
TOK = 128
EXPIRED = 4
BLOCKS = 64
NX, NZ = 4, 16
NR = 8
NC = 8
QROWS = 2 * TOK + 16
OROWS = 4 * DH + 16
KVROWS = 8 * TOK + 16
NEG = -1e30
FLOOR = -1e29
LOG2_SCALE = DH**-0.5 * 1.4426950408889634

R_GROUPS = [[x * NZ + 2 * r + par for r in range(NR)] for x in range(NX) for par in range(2)]
C_GROUPS = [[x * NZ + 2 * k + par for x in range(NX) for par in range(2)] for k in range(NZ // 2)]

NT = (((1,), (1,)), ((), ()))
NN = (((1,), (0,)), ((), ()))


def dot(a, b, dims):
    return lax.dot_general(a, b, dims, preferred_element_type=jnp.float32)


def split_perm():
    row = lax.broadcasted_iota(jnp.int32, (2 * TOK, 2 * TOK), 0)
    col = lax.broadcasted_iota(jnp.int32, (2 * TOK, 2 * TOK), 1)
    source = (row % TOK) * 2 + row // TOK
    return jnp.where(col == source, 1.0, 0.0).astype(jnp.bfloat16)


def query_kernel(want_hbm, fifo_hbm, q_hbm, q_hbm_out, want, fifo, q_in, q_split, rows, sems, out_sems):
    copies = [
        pltpu.make_async_copy(src, dst, sems.at[i])
        for i, (src, dst) in enumerate(((want_hbm, want), (fifo_hbm, fifo), (q_hbm, q_in)))
    ]
    for copy in copies:
        copy.start()
    perm = split_perm()
    row = lax.broadcasted_iota(jnp.int32, (16, TOK), 0)
    copies[0].wait()
    copies[1].wait()
    for c in range(NC):
        block = (c // 2) * NZ + 2 * row + c % 2
        chosen = block == want[0, 0]
        for i in range(1, 8):
            chosen = chosen | (block == want[0, i])
        live = ((block - fifo[0] + BLOCKS) & (BLOCKS - 1)) >= EXPIRED
        rows[c] = jnp.where(chosen & live, 0.0, NEG).astype(jnp.bfloat16)
    sends = [pltpu.make_async_copy(rows, q_hbm_out.at[:, pl.ds(2 * TOK, 16), :], out_sems.at[NC])]
    sends[0].start()
    copies[2].wait()
    q_split[...] = dot(perm, q_in[...], NN).astype(jnp.bfloat16)
    for c in range(NC):
        sends.append(pltpu.make_async_copy(q_split, q_hbm_out.at[c, pl.ds(0, 2 * TOK), :], out_sems.at[c]))
        sends[-1].start()
    for send in sends:
        send.wait()


def code_kernel(k_hbm, v_hbm, mk_hbm, mv_hbm, kv_out, rows_in, sems):
    copies = [
        pltpu.make_async_copy(src, rows_in.at[i], sems.at[i])
        for i, src in enumerate((k_hbm, v_hbm, mk_hbm, mv_hbm))
    ]
    for copy in copies:
        copy.start()
    perm = split_perm()
    powers = []
    for i, copy in enumerate(copies):
        copy.wait()
        rows = dot(perm, rows_in[i], NN)
        for h in range(2):
            block = rows[h * TOK : (h + 1) * TOK, :]
            if i % 2:
                block = jnp.transpose(block)
            peak = jnp.max(jnp.max(jnp.abs(block), 0, keepdims=True), 1, keepdims=True)
            power = jnp.floor(14.997 - jnp.log2(jnp.maximum(peak, 1e-30)))
            power = jnp.broadcast_to(power, (1, TOK))
            code = jnp.floor(block * jnp.exp2(power) + 0.5)
            code = jnp.clip(code, -32767.0, 32767.0).astype(jnp.int32)
            kv_out[pl.ds((i * 2 + h) * TOK, TOK), :] = code.astype(jnp.int16)
            powers.append(power)
    powers.append(jnp.zeros((8, TOK), jnp.float32))
    tile = jnp.concatenate(powers, 0).astype(jnp.int32)
    kv_out[pl.ds(8 * TOK, 16), :] = tile.astype(jnp.int16)


def tok_start(r):
    return r * TOK if isinstance(r, int) else pl.multiple_of(r * TOK, TOK)


def decode(kv_ref, keys_ref, vals_ref):
    for r in range(NR):
        power = kv_ref[r, pl.ds(8 * TOK, 16), :].astype(jnp.int32).astype(jnp.float32)
        factor = jnp.exp2(-power)
        for i in range(4):
            for h in range(2):
                code = kv_ref[r, pl.ds((i * 2 + h) * TOK, TOK), :].astype(jnp.bfloat16)
                block = code * factor[i * 2 + h : i * 2 + h + 1, :].astype(jnp.bfloat16)
                at = (i // 2) * 2 + h
                if i % 2:
                    vals_ref[at, pl.ds(0, DH), pl.ds(r * TOK, TOK)] = block
                else:
                    keys_ref[at, pl.ds(r * TOK, TOK), :] = block


def attend_kernel(
    pos_ref, q_ref, kv_ref, out_ref, keys_ref, vals_ref, s_ref, bias_ref, stat_ref, slot_ref
):
    decode(kv_ref, keys_ref, vals_ref)
    for at in range(4):
        vals_ref[at, pl.ds(DH, 16), :] = jnp.ones((16, NR * TOK), jnp.bfloat16)
    my_x, my_pair, my_par = pos_ref[0], pos_ref[1], pos_ref[2]
    ahead = lax.broadcasted_iota(jnp.int32, (TOK, 2 * TOK), 0) - lax.broadcasted_iota(
        jnp.int32, (TOK, 2 * TOK), 1
    )
    row = lax.broadcasted_iota(jnp.int32, (16, TOK), 0)
    place = jnp.where(row < NR, jnp.left_shift(1, row), 0).astype(jnp.float32)

    def run(xq, kind, blocks, mask):
        tops = []
        for h in range(2):
            at = kind * 2 + h
            q_rows = jnp.concatenate(
                [q_ref[2 * xq + par, pl.ds(h * TOK, TOK), :] for par in range(2)], 0
            )
            top = jnp.full((8, 2 * TOK), FLOOR, jnp.float32)
            for i, r in enumerate(blocks):
                s = mask(i, dot(keys_ref[at, pl.ds(tok_start(r), TOK), :], q_rows, NT))
                s = s * LOG2_SCALE
                s_ref[at, pl.ds(i * TOK, TOK), :] = s
                top = jnp.maximum(top, jnp.max(s.reshape(TOK // 8, 8, 2 * TOK), 0))
            tops.append(jnp.max(top, 0, keepdims=True))
        for h in range(2):
            at = kind * 2 + h
            top = tops[h]
            acc = jnp.zeros((DH + 16, 2 * TOK), jnp.float32)
            for i in range(0, len(blocks), 2):
                part = blocks[i : i + 2]
                e = jnp.exp2(s_ref[at, pl.ds(i * TOK, len(part) * TOK), :] - top)
                vals = jnp.concatenate([vals_ref[at, :, pl.ds(tok_start(r), TOK)] for r in part], 1)
                acc = acc + dot(vals, e.astype(jnp.bfloat16), NN)
            total = jnp.maximum(acc[DH : DH + 1, :], 1e-30)
            acc = (acc[:DH, :] * (1.0 / total)).astype(jnp.bfloat16)
            for par in range(2):
                out_ref[2 * xq + par, pl.ds(at * DH, DH), :] = acc[:, par * TOK : (par + 1) * TOK]
            lse = top + jnp.log2(total)
            for i in range(3):
                part = lse.astype(jnp.bfloat16).astype(jnp.float32)
                stat_ref[at * 3 + i : at * 3 + i + 1, :] = part
                lse = lse - part

    def step(xq, carry):
        def causal(r, s):
            gap = ((xq - my_x) * NZ + 2 * my_pair - 2 * r - my_par) * TOK
            return jnp.where(ahead <= gap, s, NEG)

        extra = [q_ref[2 * xq + par, pl.ds(2 * TOK, 16), :].astype(jnp.float32) for par in range(2)]
        bias_ref[...] = jnp.concatenate(extra, 1)
        wanted = jnp.where(jnp.maximum(extra[0], extra[1]) > -1.0, place, 0.0)
        bits = jnp.max(jnp.sum(wanted, 0, keepdims=True)).astype(jnp.int32)
        for r in range(NR):
            slot_ref[r] = 0
        count = jnp.int32(0)
        for r in range(NR):
            slot_ref[count] = r
            count = count + (jnp.right_shift(bits, r) & 1)

        run(xq, 0, list(range(NR)), causal)

        def some(size):
            blocks = [slot_ref[i] for i in range(size)]

            def retrieved(i, s):
                return s + jnp.where(i < count, bias_ref[pl.ds(blocks[i], 1), :], NEG)

            run(xq, 1, blocks, retrieved)

        @pl.when(count <= 2)
        def _():
            some(2)

        @pl.when((count > 2) & (count <= 4))
        def _():
            some(4)

        @pl.when(count > 4)
        def _():
            some(8)

        tile = stat_ref[...].astype(jnp.bfloat16)
        for par in range(2):
            out_ref[2 * xq + par, pl.ds(4 * DH, 16), :] = tile[:, par * TOK : (par + 1) * TOK]
        return carry

    stat_ref[...] = jnp.zeros((16, 2 * TOK), jnp.float32)
    lax.fori_loop(0, NX, step, 0)


SCRATCH = [
    pltpu.VMEM((4, NR * TOK, DH), jnp.bfloat16),
    pltpu.VMEM((4, DH + 16, NR * TOK), jnp.bfloat16),
    pltpu.VMEM((4, NR * TOK, 2 * TOK), jnp.float32),
    pltpu.VMEM((16, 2 * TOK), jnp.float32),
    pltpu.VMEM((16, 2 * TOK), jnp.float32),
    pltpu.SMEM((8,), jnp.int32),
]


def merge_kernel(gate_ref, part_ref, comb_ref, sq_ref):
    stats = [part_ref[c, pl.ds(4 * DH, 16), :].astype(jnp.float32) for c in range(NC)]
    squares = jnp.zeros((1, TOK), jnp.float32)
    for h in range(2):
        merged = []
        for kind in range(2):
            at = (kind * 2 + h) * 3
            lse = [st[at : at + 1] + st[at + 1 : at + 2] + st[at + 2 : at + 3] for st in stats]
            top = lse[0]
            for one in lse[1:]:
                top = jnp.maximum(top, one)
            weight = [jnp.exp2(one - top) for one in lse]
            total = weight[0]
            for one in weight[1:]:
                total = total + one
            acc = jnp.zeros((DH, TOK), jnp.float32)
            for c in range(NC):
                rows = part_ref[c, pl.ds((kind * 2 + h) * DH, DH), :].astype(jnp.float32)
                acc = acc + rows * weight[c]
            merged.append(acc * (1.0 / total))
        gate = gate_ref[h : h + 1, :]
        comb = gate * merged[1] + (1.0 - gate) * merged[0]
        comb_ref[h] = comb
        squares = squares + jnp.sum(comb * comb, 0, keepdims=True)
    sq_ref[...] = jnp.broadcast_to(squares, (8, TOK))


def final_kernel(sq_ref, comb_ref, gain_ref, out_ref):
    mean_square = jnp.sum(sq_ref[...], 0, keepdims=True) * (1.0 / (HEADS * DH))
    scale = lax.rsqrt(mean_square + 1e-06)
    diag = lax.broadcasted_iota(jnp.int32, (DH, DH), 0) == lax.broadcasted_iota(jnp.int32, (DH, DH), 1)
    cols = []
    for h in range(2):
        gain = jnp.sum(jnp.where(diag, gain_ref[h : h + 1, :], 0.0), 1, keepdims=True)
        cols.append((comb_ref[h] * scale * gain).astype(jnp.bfloat16))
    row = lax.broadcasted_iota(jnp.int32, (2 * TOK, 2 * TOK), 0)
    col = lax.broadcasted_iota(jnp.int32, (2 * TOK, 2 * TOK), 1)
    pick = jnp.where(col == (row % 2) * TOK + row // 2, 1.0, 0.0).astype(jnp.bfloat16)
    out_ref[...] = dot(pick, jnp.concatenate(cols, 1), NT).astype(jnp.bfloat16)


VMEM = pl.BlockSpec(memory_space=pltpu.VMEM)
ANY = pl.BlockSpec(memory_space=pl.ANY)
SMEM = pl.BlockSpec(memory_space=pltpu.SMEM)
WHOLE = pltpu.CompilerParams(vmem_limit_bytes=63 * 2**20)
PARAMS = pltpu.CompilerParams(vmem_limit_bytes=40 * 2**20)


def on_device(queries, seq_keys, seq_values, memory_keys, memory_values, retrieval, fifo_head, head_gate, norm_gain):
    me = lax.axis_index("seq")
    pos = jnp.stack([me // NZ, (me % NZ) // 2, me % 2]).astype(jnp.int32)
    flat = lambda a: a.reshape(2 * TOK, DH)
    q_parts = pl.pallas_call(
        query_kernel,
        out_shape=jax.ShapeDtypeStruct((NC, QROWS, DH), jnp.bfloat16),
        in_specs=[ANY] * 3,
        out_specs=ANY,
        scratch_shapes=[
            pltpu.SMEM((1, 8), jnp.int32),
            pltpu.SMEM((1,), jnp.int32),
            pltpu.VMEM((2 * TOK, DH), jnp.bfloat16),
            pltpu.VMEM((2 * TOK, DH), jnp.bfloat16),
            pltpu.VMEM((NC, 16, TOK), jnp.bfloat16),
            pltpu.SemaphoreType.DMA((3,)),
            pltpu.SemaphoreType.DMA((NC + 1,)),
        ],
        compiler_params=WHOLE,
        name="query",
    )(retrieval, fifo_head, flat(queries))
    q_all = lax.all_to_all(q_parts, "seq", 0, 0, axis_index_groups=C_GROUPS, tiled=True)
    kv = pl.pallas_call(
        code_kernel,
        out_shape=jax.ShapeDtypeStruct((KVROWS, DH), jnp.int16),
        in_specs=[ANY] * 4,
        out_specs=VMEM,
        scratch_shapes=[
            pltpu.VMEM((4, 2 * TOK, DH), jnp.bfloat16),
            pltpu.SemaphoreType.DMA((4,)),
        ],
        compiler_params=PARAMS,
        name="code",
    )(*map(flat, (seq_keys, seq_values, memory_keys, memory_values)))
    kv_all = lax.all_gather(kv, "seq", axis_index_groups=R_GROUPS)
    parts = pl.pallas_call(
        attend_kernel,
        out_shape=jax.ShapeDtypeStruct((NC, OROWS, DH), jnp.bfloat16),
        in_specs=[SMEM, VMEM, VMEM],
        out_specs=VMEM,
        scratch_shapes=SCRATCH,
        compiler_params=PARAMS,
        name="attend",
    )(pos, q_all, kv_all)
    parts = lax.all_to_all(parts, "seq", 0, 0, axis_index_groups=C_GROUPS, tiled=True)
    gate = jnp.broadcast_to(jax.nn.sigmoid(head_gate)[:, None], (2, TOK))
    comb, squares = pl.pallas_call(
        merge_kernel,
        out_shape=(
            jax.ShapeDtypeStruct((2, DH, TOK), jnp.float32),
            jax.ShapeDtypeStruct((8, TOK), jnp.float32),
        ),
        in_specs=[VMEM, VMEM],
        out_specs=(VMEM, VMEM),
        compiler_params=PARAMS,
        name="merge",
    )(gate, parts)
    squares = lax.all_to_all(squares, "head", 0, 0, tiled=True)
    out = pl.pallas_call(
        final_kernel,
        out_shape=jax.ShapeDtypeStruct((2 * TOK, DH), jnp.bfloat16),
        in_specs=[VMEM] * 3,
        out_specs=VMEM,
        compiler_params=PARAMS,
        name="final",
    )(squares, comb, norm_gain)
    return out.reshape(TOK, 2, DH)


def solution(mesh):
    in_specs = (P("seq", "head", None),) * 5 + (P("seq", None), P(), P("head"), P("head", None))
    return jax.shard_map(
        on_device, mesh=mesh, in_specs=in_specs, out_specs=P("seq", "head", None), check_vma=False
    )
```

```python
import jax
import jax.numpy as jnp
from jax import lax
from jax.experimental import pallas as pl
from jax.experimental.pallas import tpu as pltpu
from jax.sharding import PartitionSpec as P

HEADS = 16
DH = 128
TOK = 128
EXPIRED = 4
BLOCKS = 64
NX, NZ = 4, 16
NR = 8
NC = 8
QROWS = 2 * TOK + 16
OROWS = 4 * DH + 16
KVROWS = 8 * TOK + 16
NEG = -1e30
FLOOR = -1e29
LOG2_SCALE = DH**-0.5 * 1.4426950408889634

R_GROUPS = [[x * NZ + 2 * r + par for r in range(NR)] for x in range(NX) for par in range(2)]
C_GROUPS = [[x * NZ + 2 * k + par for x in range(NX) for par in range(2)] for k in range(NZ // 2)]

NT = (((1,), (1,)), ((), ()))
NN = (((1,), (0,)), ((), ()))


def dot(a, b, dims):
    return lax.dot_general(a, b, dims, preferred_element_type=jnp.float32)


def split_perm():
    row = lax.broadcasted_iota(jnp.int32, (2 * TOK, 2 * TOK), 0)
    col = lax.broadcasted_iota(jnp.int32, (2 * TOK, 2 * TOK), 1)
    source = (row % TOK) * 2 + row // TOK
    return jnp.where(col == source, 1.0, 0.0).astype(jnp.bfloat16)


def query_kernel(want_hbm, fifo_hbm, q_hbm, q_out, want, fifo, q_in, sems):
    copies = [
        pltpu.make_async_copy(src, dst, sems.at[i])
        for i, (src, dst) in enumerate(((want_hbm, want), (fifo_hbm, fifo), (q_hbm, q_in)))
    ]
    for copy in copies:
        copy.start()
    perm = split_perm()
    row = lax.broadcasted_iota(jnp.int32, (16, TOK), 0)
    copies[0].wait()
    copies[1].wait()
    for c in range(NC):
        block = (c // 2) * NZ + 2 * row + c % 2
        chosen = block == want[0, 0]
        for i in range(1, 8):
            chosen = chosen | (block == want[0, i])
        live = ((block - fifo[0] + BLOCKS) & (BLOCKS - 1)) >= EXPIRED
        q_out[c, pl.ds(2 * TOK, 16), :] = jnp.where(chosen & live, 0.0, NEG).astype(jnp.bfloat16)
    copies[2].wait()
    q_rows = dot(perm, q_in[...], NN).astype(jnp.bfloat16)
    for c in range(NC):
        q_out[c, pl.ds(0, 2 * TOK), :] = q_rows


def code_kernel(k_hbm, v_hbm, mk_hbm, mv_hbm, kv_out, rows_in, sems):
    copies = [
        pltpu.make_async_copy(src, rows_in.at[i], sems.at[i])
        for i, src in enumerate((k_hbm, v_hbm, mk_hbm, mv_hbm))
    ]
    for copy in copies:
        copy.start()
    perm = split_perm()
    powers = []
    for i, copy in enumerate(copies):
        copy.wait()
        rows = dot(perm, rows_in[i], NN)
        for h in range(2):
            block = rows[h * TOK : (h + 1) * TOK, :]
            if i % 2:
                block = jnp.transpose(block)
            peak = jnp.max(jnp.max(jnp.abs(block), 0, keepdims=True), 1, keepdims=True)
            power = jnp.floor(14.997 - jnp.log2(jnp.maximum(peak, 1e-30)))
            power = jnp.broadcast_to(power, (1, TOK))
            code = jnp.floor(block * jnp.exp2(power) + 0.5)
            code = jnp.clip(code, -32767.0, 32767.0).astype(jnp.int32)
            kv_out[pl.ds((i * 2 + h) * TOK, TOK), :] = code.astype(jnp.int16)
            powers.append(power)
    powers.append(jnp.zeros((8, TOK), jnp.float32))
    tile = jnp.concatenate(powers, 0).astype(jnp.int32)
    kv_out[pl.ds(8 * TOK, 16), :] = tile.astype(jnp.int16)


def tok_start(r):
    return r * TOK if isinstance(r, int) else pl.multiple_of(r * TOK, TOK)


def decode(kv_ref, keys_ref, vals_ref):
    for r in range(NR):
        power = kv_ref[r, pl.ds(8 * TOK, 16), :].astype(jnp.int32).astype(jnp.float32)
        factor = jnp.exp2(-power)
        for i in range(4):
            for h in range(2):
                code = kv_ref[r, pl.ds((i * 2 + h) * TOK, TOK), :].astype(jnp.bfloat16)
                block = code * factor[i * 2 + h : i * 2 + h + 1, :].astype(jnp.bfloat16)
                at = (i // 2) * 2 + h
                if i % 2:
                    vals_ref[at, pl.ds(0, DH), pl.ds(r * TOK, TOK)] = block
                else:
                    keys_ref[at, pl.ds(r * TOK, TOK), :] = block


def attend_kernel(
    pos_ref, q_ref, kv_ref, out_ref, keys_ref, vals_ref, s_ref, bias_ref, stat_ref, slot_ref
):
    decode(kv_ref, keys_ref, vals_ref)
    for at in range(4):
        vals_ref[at, pl.ds(DH, 16), :] = jnp.ones((16, NR * TOK), jnp.bfloat16)
    my_x, my_pair, my_par = pos_ref[0], pos_ref[1], pos_ref[2]
    ahead = lax.broadcasted_iota(jnp.int32, (TOK, 2 * TOK), 0) - lax.broadcasted_iota(
        jnp.int32, (TOK, 2 * TOK), 1
    )
    row = lax.broadcasted_iota(jnp.int32, (16, TOK), 0)
    place = jnp.where(row < NR, jnp.left_shift(1, row), 0).astype(jnp.float32)

    def run(xq, kind, blocks, mask):
        tops = []
        for h in range(2):
            at = kind * 2 + h
            q_rows = jnp.concatenate(
                [q_ref[2 * xq + par, pl.ds(h * TOK, TOK), :] for par in range(2)], 0
            )
            top = jnp.full((8, 2 * TOK), FLOOR, jnp.float32)
            for i, r in enumerate(blocks):
                s = mask(i, dot(keys_ref[at, pl.ds(tok_start(r), TOK), :], q_rows, NT))
                s = s * LOG2_SCALE
                s_ref[at, pl.ds(i * TOK, TOK), :] = s
                top = jnp.maximum(top, jnp.max(s.reshape(TOK // 8, 8, 2 * TOK), 0))
            tops.append(jnp.max(top, 0, keepdims=True))
        for h in range(2):
            at = kind * 2 + h
            top = tops[h]
            acc = jnp.zeros((DH + 16, 2 * TOK), jnp.float32)
            for i in range(0, len(blocks), 2):
                part = blocks[i : i + 2]
                e = jnp.exp2(s_ref[at, pl.ds(i * TOK, len(part) * TOK), :] - top)
                vals = jnp.concatenate([vals_ref[at, :, pl.ds(tok_start(r), TOK)] for r in part], 1)
                acc = acc + dot(vals, e.astype(jnp.bfloat16), NN)
            total = jnp.maximum(acc[DH : DH + 1, :], 1e-30)
            acc = (acc[:DH, :] * (1.0 / total)).astype(jnp.bfloat16)
            for par in range(2):
                out_ref[2 * xq + par, pl.ds(at * DH, DH), :] = acc[:, par * TOK : (par + 1) * TOK]
            lse = top + jnp.log2(total)
            for i in range(3):
                part = lse.astype(jnp.bfloat16).astype(jnp.float32)
                stat_ref[at * 3 + i : at * 3 + i + 1, :] = part
                lse = lse - part

    def step(xq, carry):
        def causal(r, s):
            gap = ((xq - my_x) * NZ + 2 * my_pair - 2 * r - my_par) * TOK
            return jnp.where(ahead <= gap, s, NEG)

        extra = [q_ref[2 * xq + par, pl.ds(2 * TOK, 16), :].astype(jnp.float32) for par in range(2)]
        bias_ref[...] = jnp.concatenate(extra, 1)
        wanted = jnp.where(jnp.maximum(extra[0], extra[1]) > -1.0, place, 0.0)
        bits = jnp.max(jnp.sum(wanted, 0, keepdims=True)).astype(jnp.int32)
        for r in range(NR):
            slot_ref[r] = 0
        count = jnp.int32(0)
        for r in range(NR):
            slot_ref[count] = r
            count = count + (jnp.right_shift(bits, r) & 1)

        run(xq, 0, list(range(NR)), causal)

        def some(size):
            blocks = [slot_ref[i] for i in range(size)]

            def retrieved(i, s):
                return s + jnp.where(i < count, bias_ref[pl.ds(blocks[i], 1), :], NEG)

            run(xq, 1, blocks, retrieved)

        @pl.when(count <= 1)
        def _():
            some(1)

        @pl.when(count == 2)
        def _():
            some(2)

        @pl.when((count > 2) & (count <= 4))
        def _():
            some(4)

        @pl.when(count > 4)
        def _():
            some(8)

        tile = stat_ref[...].astype(jnp.bfloat16)
        for par in range(2):
            out_ref[2 * xq + par, pl.ds(4 * DH, 16), :] = tile[:, par * TOK : (par + 1) * TOK]
        return carry

    stat_ref[...] = jnp.zeros((16, 2 * TOK), jnp.float32)
    lax.fori_loop(0, NX, step, 0)


SCRATCH = [
    pltpu.VMEM((4, NR * TOK, DH), jnp.bfloat16),
    pltpu.VMEM((4, DH + 16, NR * TOK), jnp.bfloat16),
    pltpu.VMEM((4, NR * TOK, 2 * TOK), jnp.float32),
    pltpu.VMEM((16, 2 * TOK), jnp.float32),
    pltpu.VMEM((16, 2 * TOK), jnp.float32),
    pltpu.SMEM((8,), jnp.int32),
]


def merge_kernel(gate_ref, part_ref, comb_ref, sq_ref):
    stats = [part_ref[c, pl.ds(4 * DH, 16), :].astype(jnp.float32) for c in range(NC)]
    squares = jnp.zeros((1, TOK), jnp.float32)
    for h in range(2):
        merged = []
        for kind in range(2):
            at = (kind * 2 + h) * 3
            lse = [st[at : at + 1] + st[at + 1 : at + 2] + st[at + 2 : at + 3] for st in stats]
            top = lse[0]
            for one in lse[1:]:
                top = jnp.maximum(top, one)
            weight = [jnp.exp2(one - top) for one in lse]
            total = weight[0]
            for one in weight[1:]:
                total = total + one
            acc = jnp.zeros((DH, TOK), jnp.float32)
            for c in range(NC):
                rows = part_ref[c, pl.ds((kind * 2 + h) * DH, DH), :].astype(jnp.float32)
                acc = acc + rows * weight[c]
            merged.append(acc * (1.0 / total))
        gate = gate_ref[h : h + 1, :]
        comb = gate * merged[1] + (1.0 - gate) * merged[0]
        comb_ref[h] = comb
        squares = squares + jnp.sum(comb * comb, 0, keepdims=True)
    sq_ref[...] = jnp.broadcast_to(squares, (8, TOK))


def final_kernel(sq_ref, comb_ref, gain_ref, out_ref):
    mean_square = jnp.sum(sq_ref[...], 0, keepdims=True) * (1.0 / (HEADS * DH))
    scale = lax.rsqrt(mean_square + 1e-06)
    diag = lax.broadcasted_iota(jnp.int32, (DH, DH), 0) == lax.broadcasted_iota(jnp.int32, (DH, DH), 1)
    cols = []
    for h in range(2):
        gain = jnp.sum(jnp.where(diag, gain_ref[h : h + 1, :], 0.0), 1, keepdims=True)
        cols.append((comb_ref[h] * scale * gain).astype(jnp.bfloat16))
    row = lax.broadcasted_iota(jnp.int32, (2 * TOK, 2 * TOK), 0)
    col = lax.broadcasted_iota(jnp.int32, (2 * TOK, 2 * TOK), 1)
    pick = jnp.where(col == (row % 2) * TOK + row // 2, 1.0, 0.0).astype(jnp.bfloat16)
    out_ref[...] = dot(pick, jnp.concatenate(cols, 1), NT).astype(jnp.bfloat16)


VMEM = pl.BlockSpec(memory_space=pltpu.VMEM)
ANY = pl.BlockSpec(memory_space=pl.ANY)
SMEM = pl.BlockSpec(memory_space=pltpu.SMEM)
WHOLE = pltpu.CompilerParams(vmem_limit_bytes=63 * 2**20)
PARAMS = pltpu.CompilerParams(vmem_limit_bytes=40 * 2**20)


def on_device(queries, seq_keys, seq_values, memory_keys, memory_values, retrieval, fifo_head, head_gate, norm_gain):
    me = lax.axis_index("seq")
    pos = jnp.stack([me // NZ, (me % NZ) // 2, me % 2]).astype(jnp.int32)
    flat = lambda a: a.reshape(2 * TOK, DH)
    q_parts = pl.pallas_call(
        query_kernel,
        out_shape=jax.ShapeDtypeStruct((NC, QROWS, DH), jnp.bfloat16),
        in_specs=[ANY] * 3,
        out_specs=VMEM,
        scratch_shapes=[
            pltpu.SMEM((1, 8), jnp.int32),
            pltpu.SMEM((1,), jnp.int32),
            pltpu.VMEM((2 * TOK, DH), jnp.bfloat16),
            pltpu.SemaphoreType.DMA((3,)),
        ],
        compiler_params=WHOLE,
        name="query",
    )(retrieval, fifo_head, flat(queries))
    q_all = lax.all_to_all(q_parts, "seq", 0, 0, axis_index_groups=C_GROUPS, tiled=True)
    kv = pl.pallas_call(
        code_kernel,
        out_shape=jax.ShapeDtypeStruct((KVROWS, DH), jnp.int16),
        in_specs=[ANY] * 4,
        out_specs=VMEM,
        scratch_shapes=[
            pltpu.VMEM((4, 2 * TOK, DH), jnp.bfloat16),
            pltpu.SemaphoreType.DMA((4,)),
        ],
        compiler_params=PARAMS,
        name="code",
    )(*map(flat, (seq_keys, seq_values, memory_keys, memory_values)))
    kv_all = lax.all_gather(kv, "seq", axis_index_groups=R_GROUPS)
    parts = pl.pallas_call(
        attend_kernel,
        out_shape=jax.ShapeDtypeStruct((NC, OROWS, DH), jnp.bfloat16),
        in_specs=[SMEM, VMEM, VMEM],
        out_specs=VMEM,
        scratch_shapes=SCRATCH,
        compiler_params=PARAMS,
        name="attend",
    )(pos, q_all, kv_all)
    parts = lax.all_to_all(parts, "seq", 0, 0, axis_index_groups=C_GROUPS, tiled=True)
    gate = jnp.broadcast_to(jax.nn.sigmoid(head_gate)[:, None], (2, TOK))
    comb, squares = pl.pallas_call(
        merge_kernel,
        out_shape=(
            jax.ShapeDtypeStruct((2, DH, TOK), jnp.float32),
            jax.ShapeDtypeStruct((8, TOK), jnp.float32),
        ),
        in_specs=[VMEM, VMEM],
        out_specs=(VMEM, VMEM),
        compiler_params=PARAMS,
        name="merge",
    )(gate, parts)
    squares = lax.all_to_all(squares, "head", 0, 0, tiled=True)
    out = pl.pallas_call(
        final_kernel,
        out_shape=jax.ShapeDtypeStruct((2 * TOK, DH), jnp.bfloat16),
        in_specs=[VMEM] * 3,
        out_specs=VMEM,
        compiler_params=PARAMS,
        name="final",
    )(squares, comb, norm_gain)
    return out.reshape(TOK, 2, DH)


def solution(mesh):
    in_specs = (P("seq", "head", None),) * 5 + (P("seq", None), P(), P("head"), P("head", None))
    return jax.shard_map(
        on_device, mesh=mesh, in_specs=in_specs, out_specs=P("seq", "head", None), check_vma=False
    )
```
